32 devices in a mesh: subset: 2 (over x), tile: 16 (over z, y, core).
Axes of the slice: x: 2, y: 2, z: 4, core: 2. Of those that a mesh axis runs over, the one named last changes fastest.
Arguments:
- images: float32 [64, 32768], P('subset', 'tile'), may hold values from 0.5 to 2
- system_tiles: bfloat16 [2, 512, 128, 128], P('subset', 'tile'), may hold values from 5.197525e-05 to 0.0025939941
- tile_vox: int32 [2, 512], P('subset', 'tile'), may hold values from 0 to 15, as said below
- tile_ray: int32 [2, 512], P('subset', 'tile'), may hold values from 0 to 15, as said below
- live_blocks: int32 [2, 16], P('subset', 'tile'), may hold values from 1 to 1, as said below
- counts: int32 [2, 64, 2048], P('subset', None, 'tile'), may hold values from 1 to 7
Outputs:
- updated: float32 [64, 32768], P('subset', 'tile')
The draws below stay inside these ranges and needn't reach their ends.
Inputs may be any that keep to these rules, and one draw needn't show every extreme that they name: `tile_vox`: within each image tile and subset, the first 16 tile slots name every voxel block of that image tile once. `tile_ray`: in each subset every ray block is named by one of the first 1 tile slots of some image tile. `live_blocks`: slots in use are the first ones of an image tile; in every draw some image tile uses all of its blocks.
All inputs are finite; a program needn't handle non-finite values.
Results may differ from the reference program's by a relative error of at most 0.00063.
Values may be sent and summed in bfloat16 or wider, within the bound.
No kernel may reach another device: no remote copies, remote signals or barrier semaphores. Data moves between devices by JAX's collectives and lax.ppermute only.
A program may use at most 64 MiB of HBM per device.

```python
import math
import jax
import jax.numpy as jnp
from jax import lax

BLOCK = 128
VB_DEV = 16
RB_DEV = 1
TILES_DEV = 32
TILE_GROUP = 32
FP = 32
ROUNDS = 4
SUBSETS = 2
TILE_DEVS = 16
RB_TOTAL = 16
VOXELS = 32768
FRAMES = 64
TILES_ALL = 512
N_SUBSET = 2
N_TILE = 16


def draw_tile_vox(key, part):
    first_key, other_key = jax.random.split(jax.random.fold_in(key, 11))
    key_list = jax.random.split(first_key, SUBSETS * TILE_DEVS)
    leading = jax.vmap(lambda single: jax.random.permutation(single, VB_DEV))(key_list)
    remaining = jax.random.randint(other_key, (SUBSETS * TILE_DEVS, TILES_DEV - VB_DEV), 0, VB_DEV)
    joined = jnp.concatenate([leading.astype(jnp.int32), remaining.astype(jnp.int32)], axis=1)
    return joined.reshape(SUBSETS, TILE_DEVS * TILES_DEV)


def draw_tile_ray(key, part):
    first_key, other_key = jax.random.split(jax.random.fold_in(key, 23))
    key_list = jax.random.split(first_key, SUBSETS)
    leading = jax.vmap(lambda single: jax.random.permutation(single, RB_TOTAL))(key_list)
    leading = leading.reshape(SUBSETS, TILE_DEVS, RB_DEV).astype(jnp.int32)
    remaining = jax.random.randint(other_key, (SUBSETS, TILE_DEVS, TILES_DEV - RB_DEV), 0, RB_TOTAL)
    joined = jnp.concatenate([leading, remaining.astype(jnp.int32)], axis=2)
    return joined.reshape(SUBSETS, TILE_DEVS * TILES_DEV)


def draw_live_blocks(key, part):
    first_key, other_key = jax.random.split(jax.random.fold_in(key, 37))
    largest = TILES_DEV // TILE_GROUP
    lowest = max(1, largest // 2)
    filled = jax.random.randint(first_key, (SUBSETS * TILE_DEVS,), lowest, largest + 1).astype(jnp.int32)
    picked = jax.random.randint(other_key, (), 0, SUBSETS * TILE_DEVS)
    filled = filled.at[picked].set(largest)
    return filled.astype(jnp.int32).reshape(SUBSETS, TILE_DEVS)


def set_ends(result, own_key, least, top_value):
    longest = result.shape.index(max(result.shape))
    spots = []
    for shift in (0, 1):
        where = [jax.random.randint(jax.random.fold_in(own_key, axis), (), 0, length) for axis, length in enumerate(result.shape)]
        where[longest] = (where[longest] + shift) % result.shape[longest]
        spots.append(tuple(where))
    return result.at[spots[0]].set(least).at[spots[1]].set(top_value)


def steps_of(stream_key, extent, shards, least, high):
    def one(axis_at, shards_of):
        heights = jax.random.uniform(jax.random.fold_in(jax.random.fold_in(stream_key, 6), axis_at), (shards_of,), jnp.float32, least / len(shards), high / len(shards))
        return jnp.repeat(jnp.exp(heights), extent[axis_at] // shards_of).reshape((-1,) + (1,) * (len(extent) - axis_at - 1))

    loudness = one(*shards[0])
    for cut in shards[1:]:
        loudness = loudness * one(*cut)
    return loudness


def setup_inputs(seed: int = 0) -> dict:
    splits = jax.random.split(jax.random.key(seed), 7)
    images = jnp.clip(jnp.exp(math.log(2.0) - 1.3862944 * jax.random.uniform(splits[0], (FRAMES, VOXELS), jnp.float32) ** steps_of(splits[0], (FRAMES, VOXELS), ((0, 2), (1, 16)), -0.2, 0.2)), 0.5, 2.0)
    system_tiles = jnp.clip(jnp.exp(math.log(0.0025939941) - 3.9101865 * jax.random.uniform(splits[1], (SUBSETS, TILES_ALL, BLOCK, BLOCK), jnp.float32) ** steps_of(splits[1], (SUBSETS, TILES_ALL, BLOCK, BLOCK), ((0, 2), (1, 16)), -0.2, 0.2)), 5.1975250244140625e-05, 0.0025939941).astype(jnp.bfloat16)
    tile_vox = draw_tile_vox(jax.random.fold_in(splits[6], 71), 0)
    tile_ray = draw_tile_ray(jax.random.fold_in(splits[6], 71), 0)
    live_blocks = draw_live_blocks(jax.random.fold_in(splits[6], 71), 0)
    counts = set_ends(jax.random.randint(splits[5], (SUBSETS, FRAMES, RB_TOTAL * BLOCK), 1, 8), jax.random.fold_in(splits[5], 1), 1, 7).astype(jnp.int32)
    return {"images": images, "system_tiles": system_tiles, "tile_vox": tile_vox, "tile_ray": tile_ray, "live_blocks": live_blocks, "counts": counts}


HIGHEST = lax.Precision.HIGHEST


def group_pass(panel, system_tiles, tile_vox, tile_ray, live_blocks, counts_now):
    tile_set = system_tiles.reshape(N_TILE, TILES_DEV, BLOCK, BLOCK)
    voxel_index = tile_vox.reshape(N_TILE, TILES_DEV).astype(jnp.int32)
    ray_index = tile_ray.reshape(N_TILE, TILES_DEV).astype(jnp.int32)
    panel_tiles = panel.reshape(FP, N_TILE, VB_DEV, BLOCK).transpose(1, 0, 2, 3)
    slot_groups = jnp.arange(TILES_DEV, dtype=jnp.int32) // TILE_GROUP
    ray_ids = jnp.arange(RB_TOTAL, dtype=jnp.int32)
    vox_ids = jnp.arange(VB_DEV, dtype=jnp.int32)

    def forward(running, entry):
        panel_dev, tiles_dev, vox_dev, ray_dev, live_dev = entry
        tile_mask = (slot_groups < live_dev).astype(jnp.float32)
        lowered = panel_dev.astype(jnp.bfloat16)
        chosen = jnp.take(lowered, vox_dev, axis=1).astype(jnp.float32)
        contrib = jnp.einsum('ftv,trv->tfr', chosen, tiles_dev.astype(jnp.float32))
        contrib = contrib * tile_mask[:, None, None]
        onehot = (ray_dev[None, :] == ray_ids[:, None]).astype(jnp.float32)
        return running + jnp.einsum('bt,tfr->fbr', onehot, contrib, precision=HIGHEST), None

    projected, _ = lax.scan(forward, jnp.zeros((FP, RB_TOTAL, BLOCK), jnp.float32),
                            (panel_tiles, tile_set, voxel_index, ray_index, live_blocks))
    ratios = (counts_now.astype(jnp.float32).reshape(FP, RB_TOTAL, BLOCK) / projected).astype(jnp.bfloat16)

    def backward(entry):
        panel_dev, tiles_dev, vox_dev, ray_dev, live_dev = entry
        tile_mask = (slot_groups < live_dev).astype(jnp.float32)
        tiles_wide = tiles_dev.astype(jnp.float32)
        chosen = jnp.take(ratios, ray_dev, axis=1).astype(jnp.float32)
        contrib = jnp.einsum('ftr,trv->tfv', chosen, tiles_wide) * tile_mask[:, None, None]
        onehot = (vox_dev[None, :] == vox_ids[:, None]).astype(jnp.float32)
        back_sum = jnp.einsum('ct,tfv->fcv', onehot, contrib, precision=HIGHEST)
        column = jnp.sum(tiles_wide, axis=1) * tile_mask[:, None]
        sensitivity = jnp.einsum('ct,tv->cv', onehot, column, precision=HIGHEST)
        return panel_dev * back_sum / sensitivity[None]

    updated = lax.map(backward, (panel_tiles, tile_set, voxel_index, ray_index, live_blocks))
    return updated.transpose(1, 0, 2, 3).reshape(FP, VOXELS)


def reference(images, system_tiles, tile_vox, tile_ray, live_blocks, counts):
    held = images.reshape(N_SUBSET, FP, VOXELS)
    group_ids = jnp.arange(N_SUBSET, dtype=jnp.int32)
    measured = counts.reshape(N_SUBSET, N_SUBSET, FP, RB_TOTAL * BLOCK)
    stepper = jax.vmap(group_pass)
    for round_index in range(ROUNDS):
        panel_ids = ((group_ids - round_index) % N_SUBSET).astype(jnp.int32)
        counts_now = measured[group_ids, panel_ids]
        held = stepper(held, system_tiles, tile_vox, tile_ray, live_blocks, counts_now)
        if round_index + 1 < ROUNDS:
            held = jnp.roll(held, 1, axis=0)
    return held.reshape(FRAMES, VOXELS)
```

```python
import jax
import jax.numpy as jnp
from jax import lax
from jax.experimental import pallas as pl
from jax.experimental.pallas import tpu as pltpu
from jax.sharding import PartitionSpec as P

TILE_GROUP = 32
ROUNDS = 4
VMEM_LIMIT = 40 * 1024 * 1024


def whole_vmem():
    return pl.BlockSpec(memory_space=pltpu.VMEM)


def whole_smem():
    return pl.BlockSpec(memory_space=pltpu.SMEM)


def project_kernel(vox_ref, ray_ref, live_ref, panel_ref, tiles_ref, out_ref, low, acc):
    blocks, _, size = low.shape
    slots = tiles_ref.shape[0]
    for b in range(blocks):
        low[b] = panel_ref[:, b * size:(b + 1) * size].astype(jnp.bfloat16)
    acc[...] = jnp.zeros_like(acc)
    live = live_ref[0, 0]
    for group in range(max(1, slots // TILE_GROUP)):

        @pl.when(group < live)
        def _():
            for t in range(group * TILE_GROUP, min(slots, (group + 1) * TILE_GROUP)):
                part = lax.dot_general(
                    low[vox_ref[0, t]], tiles_ref[t], (((1,), (1,)), ((), ())),
                    preferred_element_type=jnp.float32)
                ray = ray_ref[0, t]
                acc[ray] = acc[ray] + part

    out_ref[...] = acc[...].astype(out_ref.dtype)


def update_kernel(vox_ref, ray_ref, live_ref, ratios_ref, panel_ref, tiles_ref, out_ref, acc, sens):
    blocks, _, size = acc.shape
    slots = tiles_ref.shape[0]
    acc[...] = jnp.zeros_like(acc)
    sens[...] = jnp.zeros_like(sens)
    live = live_ref[0, 0]
    ones = jnp.ones((16, size), jnp.bfloat16)
    for group in range(max(1, slots // TILE_GROUP)):

        @pl.when(group < live)
        def _():
            for t in range(group * TILE_GROUP, min(slots, (group + 1) * TILE_GROUP)):
                tile = tiles_ref[t]
                rows = jnp.concatenate([ratios_ref[ray_ref[0, t]], ones], axis=0)
                part = jnp.dot(rows, tile, preferred_element_type=jnp.float32)
                frames = acc.shape[1]
                vox = vox_ref[0, t]
                acc[vox] = acc[vox] + part[:frames]
                sens[vox] = sens[vox] + part[frames:frames + 8]

    for b in range(blocks):
        cols = slice(b * size, (b + 1) * size)
        out_ref[:, cols] = panel_ref[:, cols] * acc[b] / sens[b][:1]


def shards(images, system_tiles, tile_vox, tile_ray, live_blocks, counts):
    frames = images.shape[0]
    size = system_tiles.shape[-1]
    vox_blocks = images.shape[1] // size
    tiles = system_tiles[0]
    measured = counts[0]
    tile_devs = lax.axis_size("tile")
    rb_dev = measured.shape[1] // size
    ray_blocks = rb_dev * tile_devs
    subset_count = lax.axis_size("subset")
    position = lax.axis_index("subset")
    params = pltpu.CompilerParams(vmem_limit_bytes=VMEM_LIMIT)
    project = pl.pallas_call(
        project_kernel,
        out_shape=jax.ShapeDtypeStruct((ray_blocks, frames, size), jnp.bfloat16),
        in_specs=[whole_smem()] * 3 + [whole_vmem()] * 2,
        out_specs=whole_vmem(),
        scratch_shapes=[pltpu.VMEM((vox_blocks, frames, size), jnp.bfloat16),
                        pltpu.VMEM((ray_blocks, frames, size), jnp.float32)],
        compiler_params=params)
    update = pl.pallas_call(
        update_kernel,
        out_shape=jax.ShapeDtypeStruct(images.shape, jnp.float32),
        in_specs=[whole_smem()] * 3 + [whole_vmem()] * 3,
        out_specs=whole_vmem(),
        scratch_shapes=[pltpu.VMEM((vox_blocks, frames, size), jnp.float32),
                        pltpu.VMEM((vox_blocks, 8, size), jnp.float32)],
        compiler_params=params)
    panel = images
    for r in range(ROUNDS):
        panel_index = (position - r) % subset_count
        now = lax.dynamic_slice_in_dim(measured, panel_index * frames, frames, 0)
        now = now.astype(jnp.float32).reshape(frames, rb_dev, size).transpose(1, 0, 2)
        partial = project(tile_vox, tile_ray, live_blocks, panel, tiles)
        got = lax.all_to_all(partial, "tile", 0, 0, tiled=True)
        sums = got.reshape(tile_devs, rb_dev, frames, size).astype(jnp.float32).sum(0)
        ratios = (now / sums).astype(jnp.bfloat16)
        spread = jnp.broadcast_to(ratios[None], (tile_devs,) + ratios.shape)
        all_ratios = lax.all_to_all(spread.reshape(ray_blocks, frames, size), "tile", 0, 0, tiled=True)
        panel = update(tile_vox, tile_ray, live_blocks, all_ratios, panel, tiles)
        if r + 1 < ROUNDS:
            panel = lax.ppermute(panel, "subset", [(i, (i + 1) % subset_count) for i in range(subset_count)])
    return panel


def solution(mesh):
    in_specs = (
        P("subset", "tile"),
        P("subset", "tile", None, None),
        P("subset", "tile"),
        P("subset", "tile"),
        P("subset", "tile"),
        P("subset", None, "tile"),
    )
    return jax.shard_map(shards, mesh=mesh, in_specs=in_specs, out_specs=P("subset", "tile"),
                         check_vma=False)
```

```python
import functools

import jax
import jax.numpy as jnp
from jax import lax
from jax.experimental import pallas as pl
from jax.experimental.pallas import tpu as pltpu
from jax.sharding import PartitionSpec as P

TILE_GROUP = 32
ROUNDS = 4
CORES = 2
LANES = 128
VMEM_LIMIT = 40 * 1024 * 1024


def vmem():
    return pl.BlockSpec(memory_space=pltpu.VMEM)


def smem():
    return pl.BlockSpec(memory_space=pltpu.SMEM)


def each_live(index_ref, slots, body):
    live = index_ref[2, 0]
    for group in range(-(-slots // TILE_GROUP)):

        @pl.when(group < live)
        def _():
            for t in range(group * TILE_GROUP, min(slots, (group + 1) * TILE_GROUP)):
                body(t)


def project_kernel(*refs):
    index_refs, low_ref, tile_refs, (out_ref, low, acc) = refs[:2], refs[2], refs[3:5], refs[5:]
    size = low.shape[-1]
    blocks = low.shape[0] // CORES
    for k in range(CORES):
        for b in range(blocks):
            low[k * blocks + b] = low_ref[k, :, b * size:(b + 1) * size].astype(jnp.bfloat16)
    acc[...] = jnp.zeros_like(acc)
    for k in range(CORES):
        index_ref, tiles_ref = index_refs[k], tile_refs[k]

        def body(t):
            part = lax.dot_general(low[k * blocks + index_ref[0, t]], tiles_ref[t],
                                   (((1,), (1,)), ((), ())), preferred_element_type=jnp.float32)
            ray = index_ref[1, t]
            acc[ray] = acc[ray] + part

        each_live(index_ref, tiles_ref.shape[0], body)
    out_ref[...] = acc[...].astype(out_ref.dtype)


def sensitivity_kernel(*refs):
    index_refs, tile_refs, (out_ref, acc) = refs[:2], refs[2:4], refs[4:]
    blocks = acc.shape[0] // CORES
    acc[...] = jnp.zeros_like(acc)
    ones = jnp.ones((16, tile_refs[0].shape[1]), jnp.bfloat16)
    for k in range(CORES):
        index_ref, tiles_ref = index_refs[k], tile_refs[k]

        def body(t):
            part = jnp.dot(ones, tiles_ref[t], preferred_element_type=jnp.float32)
            at = k * blocks + index_ref[0, t]
            acc[at] = acc[at] + part[:8]

        each_live(index_ref, tiles_ref.shape[0], body)
    out_ref[...] = 1.0 / acc[...]


def update_kernel(held_parts, *refs):
    index_refs, ratios_ref = refs[:2], refs[2]
    held_refs, rest = refs[3:3 + held_parts], refs[3 + held_parts:]
    inverse_ref, tile_refs, out_refs, acc = rest[0], rest[1:3], rest[3:-1], rest[-1]

    def held_of(k, cols):
        return sum(ref[k, :, cols].astype(jnp.float32) for ref in held_refs)

    size = acc.shape[-1]
    blocks = acc.shape[0] // CORES
    acc[...] = jnp.zeros_like(acc)
    for k in range(CORES):
        index_ref, tiles_ref = index_refs[k], tile_refs[k]

        def body(t):
            part = jnp.dot(ratios_ref[index_ref[1, t]], tiles_ref[t],
                           preferred_element_type=jnp.float32)
            at = k * blocks + index_ref[0, t]
            acc[at] = acc[at] + part

        each_live(index_ref, tiles_ref.shape[0], body)
    for k in range(CORES):
        for b in range(blocks):
            cols = slice(b * size, (b + 1) * size)
            at = k * blocks + b
            value = held_of(k, cols) * acc[at] * inverse_ref[at, :1]
            high = value.astype(out_refs[0].dtype)
            out_refs[0][k, :, cols] = high
            if len(out_refs) == 2:
                out_refs[1][k, :, cols] = (value - high.astype(jnp.float32)).astype(jnp.bfloat16)


def call(kernel, ins, out_shape, scratch):
    return pl.pallas_call(
        kernel,
        out_shape=out_shape,
        in_specs=[smem()] * CORES + [vmem()] * (len(ins) - CORES),
        out_specs=jax.tree.map(lambda _: vmem(), out_shape),
        scratch_shapes=scratch,
        compiler_params=pltpu.CompilerParams(vmem_limit_bytes=VMEM_LIMIT))(*ins)


def shards(images, system_tiles, tile_vox, tile_ray, live_blocks, counts):
    frames = images.shape[0]
    half = frames // CORES
    size = system_tiles.shape[-1]
    voxels = images.shape[1]
    vox_blocks = voxels // size
    own_tiles = system_tiles[0]
    slots = own_tiles.shape[0]
    measured = counts[0]
    tile_devs = lax.axis_size("tile")
    peers = tile_devs // CORES
    rb_dev = measured.shape[1] // size
    rb_chip = rb_dev * CORES
    ray_blocks = rb_dev * tile_devs
    subset_count = lax.axis_size("subset")
    position = lax.axis_index("subset")
    core = lax.axis_index("tile") % CORES
    swap = [(i, i ^ 1) for i in range(tile_devs)]
    groups = [[c + CORES * j for j in range(peers)] for c in range(CORES)]
    shift = [(i, (i + 1) % subset_count) for i in range(subset_count)]

    width = -(-slots // LANES) * LANES
    rows = jnp.concatenate([tile_vox, tile_ray, jnp.broadcast_to(live_blocks, tile_vox.shape)], axis=0)
    index_own = jnp.pad(rows, ((0, 5), (0, width - slots)))
    halves = images.reshape(CORES, half, voxels)
    counts_halves = measured.reshape(subset_count, CORES, half, rb_dev * size)
    mine = lax.dynamic_index_in_dim(halves, core, 0, keepdims=False)
    theirs = lax.dynamic_index_in_dim(halves, 1 - core, 0, keepdims=False)
    counts_mine = lax.dynamic_index_in_dim(counts_halves, core, 1, keepdims=False)
    counts_theirs = lax.dynamic_index_in_dim(counts_halves, 1 - core, 1, keepdims=False)
    other_half = lax.ppermute(theirs, "tile", swap)
    other_tiles = lax.ppermute(own_tiles, "tile", swap)
    index_other = lax.ppermute(index_own, "tile", swap)
    counts_other = lax.ppermute(counts_theirs, "tile", swap)
    counts_both = jnp.where(core == 0, jnp.stack([counts_mine, counts_other]),
                            jnp.stack([counts_other, counts_mine]))
    counts_both = counts_both.reshape(CORES, subset_count, half, rb_dev, size)
    counts_both = counts_both.transpose(1, 0, 3, 2, 4).reshape(subset_count, rb_chip, half, size)
    counts_both = counts_both.astype(jnp.float32)

    held = jnp.stack([mine, other_half])
    index = (index_own, index_other)
    tiles = (own_tiles, other_tiles)
    both = CORES * vox_blocks
    inverse = call(sensitivity_kernel, (*index, *tiles),
                   jax.ShapeDtypeStruct((both, 8, size), jnp.float32),
                   [pltpu.VMEM((both, 8, size), jnp.float32)])
    state = (held,)
    for r in range(ROUNDS):
        now = lax.dynamic_index_in_dim(counts_both, (position - r) % subset_count, 0, keepdims=False)
        partial = call(project_kernel, (*index, state[0], *tiles),
                       jax.ShapeDtypeStruct((ray_blocks, half, size), jnp.bfloat16),
                       [pltpu.VMEM((both, half, size), jnp.bfloat16),
                        pltpu.VMEM((ray_blocks, half, size), jnp.float32)])
        got = lax.all_to_all(partial, "tile", 0, 0, axis_index_groups=groups, tiled=True)
        sums = got.reshape(peers, rb_chip, half, size).astype(jnp.float32).sum(0)
        ratios = (now / sums).astype(jnp.bfloat16)
        spread = jnp.broadcast_to(ratios[None], (peers,) + ratios.shape)
        all_ratios = lax.all_to_all(spread.reshape(ray_blocks, half, size), "tile", 0, 0,
                                    axis_index_groups=groups, tiled=True)
        last = r + 1 == ROUNDS
        shape = (CORES, half, voxels)
        out_shape = (jax.ShapeDtypeStruct(shape, jnp.float32) if last else
                     (jax.ShapeDtypeStruct(shape, jnp.bfloat16),) * 2)
        state = call(functools.partial(update_kernel, len(state)), (*index, all_ratios, *state, inverse, *tiles), out_shape,
                     [pltpu.VMEM((both, half, size), jnp.float32)])
        if not last:
            high = lax.ppermute(state[0], "subset", shift)
            low, _ = lax.optimization_barrier((state[1], high))
            state = (high, lax.ppermute(low, "subset", shift))
    back_half = lax.ppermute(state[1], "tile", swap)
    return jnp.where(core == 0, jnp.concatenate([state[0], back_half]),
                     jnp.concatenate([back_half, state[0]]))


def solution(mesh):
    in_specs = (
        P("subset", "tile"),
        P("subset", "tile", None, None),
        P("subset", "tile"),
        P("subset", "tile"),
        P("subset", "tile"),
        P("subset", None, "tile"),
    )
    return jax.shard_map(shards, mesh=mesh, in_specs=in_specs, out_specs=P("subset", "tile"),
                         check_vma=False)
```

```python
import jax
import jax.numpy as jnp
from jax import lax
from jax.experimental import pallas as pl
from jax.experimental.pallas import tpu as pltpu
from jax.sharding import PartitionSpec as P

TILE_GROUP = 32
ROUNDS = 4
CORES = 2
LANES = 128
VMEM_LIMIT = 40 * 1024 * 1024


def each_live(index_ref, slots, body):
    live = index_ref[2, 0]
    for group in range(-(-slots // TILE_GROUP)):
        first, last = group * TILE_GROUP, min(slots, (group + 1) * TILE_GROUP)

        @pl.when(group < live)
        def _():
            for t in range(first, last, 2):
                body(tuple(range(t, min(t + 2, last))))


def add_products(acc, left_of, targets, wide, transposed):
    left = jnp.concatenate(left_of, axis=0)
    dims = (((1,), (1,)), ((), ())) if transposed else (((1,), (0,)), ((), ()))
    part = lax.dot_general(left, wide, dims, preferred_element_type=jnp.float32)
    rows, size = acc.shape[1:]
    for i, at in enumerate(targets):
        used = part[i * left_of[i].shape[0]:, i * size:(i + 1) * size][:rows]
        acc[at] = acc[at] + used


def project_into(acc, low, index_refs, tile_refs):
    blocks = low.shape[0] // CORES
    acc[...] = jnp.zeros_like(acc)
    for k in range(CORES):
        index_ref, tiles_ref = index_refs[k], tile_refs[k]

        def body(ts):
            wide = jnp.concatenate([tiles_ref[t] for t in ts], axis=0)
            add_products(acc, [low[k * blocks + index_ref[0, t]] for t in ts],
                         [index_ref[1, t] for t in ts], wide, True)

        each_live(index_ref, tiles_ref.shape[0], body)


def back_into(acc, ratios, index_refs, tile_refs):
    blocks = acc.shape[0] // CORES
    acc[...] = jnp.zeros_like(acc)
    for k in range(CORES):
        index_ref, tiles_ref = index_refs[k], tile_refs[k]

        def body(ts):
            wide = jnp.concatenate([tiles_ref[t] for t in ts], axis=1)
            add_products(acc, [ratios(index_ref[1, t]) for t in ts],
                         [k * blocks + index_ref[0, t] for t in ts], wide, False)

        each_live(index_ref, tiles_ref.shape[0], body)


def columns(blocks, size):
    for k in range(CORES):
        for b in range(blocks):
            yield k, slice(b * size, (b + 1) * size), k * blocks + b


def project_kernel(ins, outs, low, acc):
    blocks, size = low.shape[0] // CORES, low.shape[-1]
    for k, cols, at in columns(blocks, size):
        low[at] = ins["held"][k][:, cols].astype(jnp.bfloat16)
    project_into(acc, low, ins["index"], ins["tiles"])
    outs["wide"][...] = acc[...]
    outs["sent"][...] = acc[...].astype(jnp.bfloat16)


def sensitivity_kernel(ins, outs, acc):
    ones = jnp.ones((16, ins["tiles"][0].shape[1]), jnp.bfloat16)
    back_into(acc, lambda ray: ones, ins["index"], ins["tiles"])
    outs["inverse"][...] = 1.0 / acc[...]


def update_kernel(ins, outs, ratios, back, *scratch):
    blocks, size = back.shape[0] // CORES, back.shape[-1]
    total = ins["wide"][...] + ins["got"][...].astype(jnp.float32)
    ratios[...] = (ins["counts"][...].astype(jnp.float32) / total).astype(jnp.bfloat16)
    back_into(back, lambda ray: ratios[ray], ins["index"], ins["tiles"])
    for k, cols, at in columns(blocks, size):
        held = sum(part[k][:, cols].astype(jnp.float32) for part in ins["held"])
        value = held * back[at] * ins["inverse"][at, :1]
        high = value.astype(jnp.bfloat16)
        if "high" in outs:
            outs["high"][k, :, cols] = high
            outs["low"][k, :, cols] = (value - high.astype(jnp.float32)).astype(jnp.bfloat16)
        else:
            outs["held"][k, :, cols] = value
        if "sent" in outs:
            scratch[0][at] = high
    if "sent" in outs:
        project_into(scratch[1], scratch[0], ins["next_index"], ins["next_tiles"])
        outs["wide"][...] = scratch[1][...]
        outs["sent"][...] = scratch[1][...].astype(jnp.bfloat16)


def call(kernel, ins, outs, scratch):
    def spec(path, _):
        name = path[0].key
        return pl.BlockSpec(memory_space=pltpu.SMEM if name.endswith("index") else pltpu.VMEM)

    return pl.pallas_call(
        kernel,
        out_shape=outs,
        in_specs=[jax.tree_util.tree_map_with_path(spec, ins)],
        out_specs=jax.tree_util.tree_map_with_path(spec, outs),
        scratch_shapes=scratch,
        compiler_params=pltpu.CompilerParams(vmem_limit_bytes=VMEM_LIMIT))(ins)


def shards(images, system_tiles, tile_vox, tile_ray, live_blocks, counts):
    frames, voxels = images.shape
    half = frames // CORES
    size = system_tiles.shape[-1]
    vox_blocks = voxels // size
    own_tiles = system_tiles[0]
    slots = own_tiles.shape[0]
    tile_devs = lax.axis_size("tile")
    chips = tile_devs // CORES
    rb_dev = counts.shape[2] // size
    ray_blocks = rb_dev * tile_devs
    subset_count = lax.axis_size("subset")
    position = lax.axis_index("subset")
    core = lax.axis_index("tile") % CORES
    both = CORES * vox_blocks
    f32, bf16 = jnp.float32, jnp.bfloat16
    shaped = jax.ShapeDtypeStruct

    def swap_cores(array):
        return lax.ppermute(array, "tile", [(i, i ^ 1) for i in range(tile_devs)])

    def swap_chips(array, step):
        pairs = [(CORES * j + c, CORES * (j ^ step) + c) for j in range(chips) for c in range(CORES)]
        return lax.ppermute(array, "tile", pairs)

    def joined(side, own, other):
        return jnp.where(side == 0, jnp.concatenate([own, other]), jnp.concatenate([other, own]))

    def shift(array):
        return lax.ppermute(array, "subset", [(i, (i + 1) % subset_count) for i in range(subset_count)])

    halves = images.reshape(CORES, half, voxels)
    mine = lax.dynamic_index_in_dim(halves, core, 0, keepdims=False)
    theirs = lax.dynamic_index_in_dim(halves, 1 - core, 0, keepdims=False)
    rows = jnp.concatenate([tile_vox, tile_ray, jnp.broadcast_to(live_blocks, tile_vox.shape)], axis=0)
    own_index = jnp.pad(rows, ((0, 5), (0, -slots % LANES)))
    tiles = (own_tiles, swap_cores(own_tiles))
    held = ((mine, swap_cores(theirs)),)
    index = (own_index, swap_cores(own_index))

    dealt = counts[0].astype(bf16).reshape(subset_count, CORES, half, rb_dev, size).transpose(1, 3, 0, 2, 4)
    kept = lax.dynamic_index_in_dim(dealt, core, 0, keepdims=False)
    got = swap_cores(lax.dynamic_index_in_dim(dealt, 1 - core, 0, keepdims=False))
    all_counts = joined(core, kept, got)
    step = 1
    while step < chips:
        side = lax.axis_index("tile") // CORES // step % 2
        all_counts = joined(side, all_counts, swap_chips(all_counts, step))
        step *= 2

    def counts_of(panel):
        return lax.dynamic_index_in_dim(all_counts, panel % subset_count, 1, keepdims=False)

    def sensitivity(index, tiles):
        return call(sensitivity_kernel, {"index": index, "tiles": tiles},
                    {"inverse": shaped((both, 8, size), f32)},
                    [pltpu.VMEM((both, 8, size), f32)])["inverse"]

    inverse = sensitivity(index, tiles)
    sets = [(index, tiles, inverse)] * ROUNDS
    moves = [True] * (ROUNDS - 1)
    now = [counts_of(position - r) for r in range(ROUNDS)]
    if subset_count == 2:
        far_index, far_tiles, far_counts = shift(own_index), shift(own_tiles), shift(now[0])
        far_index, far_tiles = (far_index, swap_cores(far_index)), (far_tiles, swap_cores(far_tiles))
        far = (far_index, far_tiles, sensitivity(far_index, far_tiles))
        for r in range(2, ROUNDS, 2):
            sets[r], now[r] = far, far_counts
        moves = [r == 0 for r in range(ROUNDS - 1)]
        if ROUNDS % 2:
            moves[-1] = True

    sums = {"wide": shaped((ray_blocks, half, size), f32), "sent": shaped((ray_blocks, half, size), bf16)}
    sum_scratch = [pltpu.VMEM((both, half, size), bf16), pltpu.VMEM((ray_blocks, half, size), f32)]

    def project(held, r):
        return call(project_kernel, {"held": held, "index": sets[r][0], "tiles": sets[r][1]},
                    sums, sum_scratch)

    out = project(held[0], 0)
    for r in range(ROUNDS):
        wide, sent = out["wide"], out["sent"]
        step = 1
        while step < chips:
            got = swap_chips(sent, step)
            step *= 2
            if step < chips:
                wide = wide + got.astype(f32)
                sent = wide.astype(bf16)
        ins = {"wide": wide, "got": got, "counts": now[r], "held": held,
               "index": sets[r][0], "tiles": sets[r][1], "inverse": sets[r][2]}
        scratch = [pltpu.VMEM((ray_blocks, half, size), bf16), pltpu.VMEM((both, half, size), f32)]
        panel = (CORES, half, voxels)
        if r + 1 == ROUNDS:
            held = call(update_kernel, ins, {"held": shaped(panel, f32)}, scratch)["held"]
        elif moves[r]:
            out = call(update_kernel, ins, {"high": shaped(panel, bf16), "low": shaped(panel, bf16)}, scratch)
            high = shift(out["high"])
            low, _ = lax.optimization_barrier((out["low"], high))
            held = (high, shift(low))
            out = project(high, r + 1)
        else:
            ins.update(next_index=sets[r + 1][0], next_tiles=sets[r + 1][1])
            out = call(update_kernel, ins, {"held": shaped(panel, f32), **sums}, scratch + sum_scratch)
            held = (out["held"],)
    return joined(core, held[0], swap_cores(held[1]))


def solution(mesh):
    in_specs = (
        P("subset", "tile"),
        P("subset", "tile", None, None),
        P("subset", "tile"),
        P("subset", "tile"),
        P("subset", "tile"),
        P("subset", None, "tile"),
    )
    return jax.shard_map(shards, mesh=mesh, in_specs=in_specs, out_specs=P("subset", "tile"),
                         check_vma=False)
```

```python
import functools

import jax
import jax.numpy as jnp
from jax import lax
from jax.experimental import pallas as pl
from jax.experimental.pallas import tpu as pltpu
from jax.sharding import PartitionSpec as P

TILE_GROUP = 32
ROUNDS = 4
CORES = 2
LANES = 128
VMEM_LIMIT = 40 * 1024 * 1024


def each_live(index_ref, slots, body):
    live = index_ref[2, 0]
    for group in range(-(-slots // TILE_GROUP)):
        first, last = group * TILE_GROUP, min(slots, (group + 1) * TILE_GROUP)

        @pl.when(group < live)
        def _():
            for t in range(first, last, 2):
                body(tuple(range(t, min(t + 2, last))))


def add_products(acc, left_of, targets, wide, transposed):
    left = jnp.concatenate(left_of, axis=0)
    dims = (((1,), (1,)), ((), ())) if transposed else (((1,), (0,)), ((), ()))
    part = lax.dot_general(left, wide, dims, preferred_element_type=jnp.float32)
    rows, size = acc.shape[1:]
    for i, at in enumerate(targets):
        used = part[i * left_of[i].shape[0]:, i * size:(i + 1) * size][:rows]
        acc[at] = acc[at] + used


def tile_at(tile_refs, t):
    for ref in tile_refs:
        if t < ref.shape[0]:
            return ref[t]
        t -= ref.shape[0]


def slots_of(tile_refs):
    return sum(ref.shape[0] for ref in tile_refs)


def project_into(acc, low, index_refs, sets):
    blocks = low.shape[0] // CORES
    for k in range(CORES):
        if sets[k] is None:
            continue
        index_ref, tile_refs = index_refs[k], sets[k]

        def body(ts):
            wide = jnp.concatenate([tile_at(tile_refs, t) for t in ts], axis=0)
            add_products(acc, [low[k * blocks + index_ref[0, t]] for t in ts],
                         [index_ref[1, t] for t in ts], wide, True)

        each_live(index_ref, slots_of(tile_refs), body)


def back_into(acc, ratios, index_refs, sets):
    blocks = acc.shape[0] // CORES
    acc[...] = jnp.zeros_like(acc)
    for k in range(CORES):
        index_ref, tile_refs = index_refs[k], sets[k]

        def body(ts):
            wide = jnp.concatenate([tile_at(tile_refs, t) for t in ts], axis=1)
            add_products(acc, [ratios(index_ref[1, t]) for t in ts],
                         [k * blocks + index_ref[0, t] for t in ts], wide, False)

        each_live(index_ref, slots_of(tile_refs), body)


def columns(blocks, size):
    for k in range(CORES):
        for b in range(blocks):
            yield k, slice(b * size, (b + 1) * size), k * blocks + b


def piece_of(held, k, cols):
    return held[k][:, cols] if isinstance(held, tuple) else held[k, :, cols]


def write_sums(ins, outs, acc):
    blocks = acc.shape[0]
    outs["wide"][...] = acc[...]
    outs["sent"][:blocks] = acc[...].astype(jnp.bfloat16)
    if "dealt" in ins:
        outs["sent"][blocks:] = ins["dealt"][...]


def first_kernel(ins, outs, low, acc, own, arrived):
    copy = pltpu.make_async_copy(ins["own_hbm"], own, arrived)
    copy.start()
    blocks, size = low.shape[0] // CORES, low.shape[-1]
    for k, cols, at in columns(blocks, size):
        low[at] = piece_of(ins["held"], k, cols).astype(jnp.bfloat16)
    acc[...] = jnp.zeros_like(acc)
    project_into(acc, low, ins["index"], (None, ins["tiles"]))
    copy.wait()
    project_into(acc, low, ins["index"], ((own,), None))
    write_sums(ins, outs, acc)


def project_kernel(ins, outs, low, acc):
    blocks, size = low.shape[0] // CORES, low.shape[-1]
    acc[...] = jnp.zeros_like(acc)
    for k, cols, at in columns(blocks, size):
        low[at] = piece_of(ins["held"], k, cols).astype(jnp.bfloat16)
    project_into(acc, low, ins["index"], ins["tiles"])
    write_sums(ins, outs, acc)


def sensitivity_kernel(ins, outs, acc):
    ones = jnp.ones((16, ins["tiles"][0][0].shape[1]), jnp.bfloat16)
    back_into(acc, lambda ray: ones, ins["index"], ins["tiles"])
    outs["inverse"][...] = 1.0 / acc[...]


def update_kernel(masks, ins, outs, counts, ratios, back, *scratch):
    blocks, size = back.shape[0] // CORES, back.shape[-1]
    rays = ratios.shape[0]
    total = ins["wide"][...]
    for got in ins["got"]:
        total = total + got[:rays].astype(jnp.float32)
    if "counts" in ins:
        counts[...] = ins["counts"][...]
    else:
        place = ins["index"][0][3, 0]
        share = ins["sent"].shape[0] - rays
        for mask, part in zip((0,) + masks, (ins["sent"],) + tuple(ins["got"])):
            counts[pl.ds((place ^ mask) * share, share)] = part[rays:]
    if "counts" in outs:
        outs["counts"][...] = counts[...]
    ratios[...] = (counts[...].astype(jnp.float32) / total).astype(jnp.bfloat16)
    back_into(back, lambda ray: ratios[ray], ins["index"], ins["tiles"])
    for k, cols, at in columns(blocks, size):
        value = piece_of(ins["held"], k, cols) * back[at] * ins["inverse"][at, :1]
        outs["held"][k, :, cols] = value
        if "sent" in outs:
            scratch[0][at] = value.astype(jnp.bfloat16)
    if "sent" in outs:
        scratch[1][...] = jnp.zeros_like(scratch[1])
        project_into(scratch[1], scratch[0], ins["next_index"], ins["next_tiles"])
        write_sums(ins, outs, scratch[1])


def call(kernel, ins, outs, scratch):
    def spec(path, _):
        name = path[0].key
        space = pltpu.SMEM if name.endswith("index") else pltpu.HBM if name.endswith("hbm") else pltpu.VMEM
        return pl.BlockSpec(memory_space=space)

    return pl.pallas_call(
        kernel,
        out_shape=outs,
        in_specs=[jax.tree_util.tree_map_with_path(spec, ins)],
        out_specs=jax.tree_util.tree_map_with_path(spec, outs),
        scratch_shapes=scratch,
        compiler_params=pltpu.CompilerParams(vmem_limit_bytes=VMEM_LIMIT))(ins)


def shards(images, system_tiles, tile_vox, tile_ray, live_blocks, counts):
    frames, voxels = images.shape
    half = frames // CORES
    size = system_tiles.shape[-1]
    vox_blocks = voxels // size
    own_tiles = system_tiles[0]
    slots = own_tiles.shape[0]
    tile_devs = lax.axis_size("tile")
    chips = tile_devs // CORES
    rb_dev = counts.shape[2] // size
    ray_blocks = rb_dev * tile_devs
    subset_count = lax.axis_size("subset")
    position = lax.axis_index("subset")
    core = lax.axis_index("tile") % CORES
    chip = lax.axis_index("tile") // CORES
    both = CORES * vox_blocks
    f32, bf16 = jnp.float32, jnp.bfloat16
    shaped = jax.ShapeDtypeStruct

    steps, bit = [(1,)], 2
    while bit < chips:
        wide_step = bit * 4 <= chips
        steps.append((bit, 3 * bit, 2 * bit) if wide_step else (bit,))
        bit *= 4 if wide_step else 2

    def place(masks):
        return chip // min(masks) % (len(masks) + 1)

    def swap_cores(array):
        return lax.ppermute(array, "tile", [(i, i ^ 1) for i in range(tile_devs)])

    def swap_chips(array, mask):
        pairs = [(CORES * j + c, CORES * (j ^ mask) + c) for j in range(chips) for c in range(CORES)]
        return lax.ppermute(array, "tile", pairs)

    def joined(side, own, other):
        return jnp.where(side == 0, jnp.concatenate([own, other]), jnp.concatenate([other, own]))

    def shift(array):
        return lax.ppermute(array, "subset", [(i, (i + 1) % subset_count) for i in range(subset_count)])

    def after(array, value):
        return lax.optimization_barrier((array, value))[0]

    halves = images.reshape(CORES, half, voxels)
    mine = lax.dynamic_index_in_dim(halves, core, 0, keepdims=False)
    theirs = lax.dynamic_index_in_dim(halves, 1 - core, 0, keepdims=False)
    rows = jnp.concatenate([tile_vox, tile_ray, jnp.broadcast_to(live_blocks, tile_vox.shape),
                            jnp.broadcast_to(place(steps[-1]), tile_vox.shape)], axis=0)
    own_index = jnp.pad(rows, ((0, 4), (0, -slots % LANES)))
    tiles = ((own_tiles,), (swap_cores(own_tiles),))
    held = (mine, swap_cores(theirs))
    index = (own_index, swap_cores(own_index))

    dealt = counts[0].astype(bf16).reshape(subset_count, CORES, half, rb_dev, size).transpose(1, 3, 0, 2, 4)
    kept = lax.dynamic_index_in_dim(dealt, core, 0, keepdims=False)
    got = swap_cores(lax.dynamic_index_in_dim(dealt, 1 - core, 0, keepdims=False))
    dealt = joined(core, kept, got)

    def dealt_of(panel):
        return lax.dynamic_index_in_dim(dealt, panel % subset_count, 1, keepdims=False)

    def sensitivity(index, tiles):
        return call(sensitivity_kernel, {"index": index, "tiles": tiles},
                    {"inverse": shaped((both, 8, size), f32)},
                    [pltpu.VMEM((both, 8, size), f32)])["inverse"]

    sets = [(index, tiles, sensitivity(index, tiles))] * ROUNDS
    moves = [True] * (ROUNDS - 1)
    known = [None] * ROUNDS
    two = subset_count == 2
    if two:
        moves = [r == 0 for r in range(ROUNDS - 1)]

    scratch_sum = [pltpu.VMEM((both, half, size), bf16), pltpu.VMEM((ray_blocks, half, size), f32)]
    scratch = [pltpu.VMEM((ray_blocks, half, size), bf16)] * 2 + [pltpu.VMEM((both, half, size), f32)]

    def sums(r):
        fresh = known[r] is None
        sent = ray_blocks + fresh * rb_dev * CORES
        return ({"dealt": dealt_of(position - r)} if fresh else {},
                {"wide": shaped((ray_blocks, half, size), f32), "sent": shaped((sent, half, size), bf16)})

    def project(held, r):
        extra, outs = sums(r)
        return call(project_kernel, {"held": held, "index": sets[r][0], "tiles": sets[r][1], **extra},
                    outs, scratch_sum)

    extra, outs = sums(0)
    out = call(first_kernel, {"held": held, "index": index, "own_hbm": own_tiles, "tiles": tiles[1], **extra},
               outs, scratch_sum + [pltpu.VMEM(own_tiles.shape, bf16), pltpu.SemaphoreType.DMA])
    for r in range(ROUNDS):
        wide, sent = out["wide"], out["sent"]
        if two and r == 0:
            far_index = shift(after(own_index, sent))
            far_tiles = [shift(after(own_tiles[:slots * 5 // 8], sent))]
        if two and r == 1:
            far_index = (far_index, swap_cores(after(far_index, sent)))
            far_swapped = [swap_cores(after(far_tiles[0], sent))]
            far_tiles.append(shift(after(own_tiles[slots * 5 // 8:], sent)))
        for masks in steps:
            got = [swap_chips(sent, mask) for mask in masks]
            if masks is not steps[-1]:
                wide = wide + sum(part[:ray_blocks].astype(f32) for part in got)
                own, counted = place(masks), wide.astype(bf16)
                if sent.shape[0] > ray_blocks:
                    parts = dict(zip((0,) + masks, [sent] + got))
                    ordered = [parts[m * min(masks)][ray_blocks:] for m in range(len(parts))]
                    if len(ordered) == 2:
                        passed = joined(own, *ordered)
                    else:
                        passed = jnp.concatenate([lax.dynamic_index_in_dim(
                            jnp.stack(ordered), own ^ v, 0, keepdims=False) for v in range(len(ordered))])
                    counted = jnp.concatenate([counted, passed])
                sent = counted
        if two and r == 1:
            far_swapped.append(swap_cores(after(far_tiles[1], tuple(got))))
            far_tiles = (tuple(far_tiles), tuple(far_swapped))
            far = (far_index, far_tiles, sensitivity(far_index, far_tiles))
            sets = [far if later >= 2 and later % 2 == 0 else sets[later] for later in range(ROUNDS)]
        ins = {"wide": wide, "got": got, "held": held,
               "index": sets[r][0], "tiles": sets[r][1], "inverse": sets[r][2]}
        outs = {"held": shaped((CORES, half, voxels), f32)}
        if known[r] is None:
            ins["sent"] = sent
            if two:
                outs["counts"] = shaped((ray_blocks, half, size), bf16)
        else:
            ins["counts"] = known[r]
        kernel = functools.partial(update_kernel, tuple(m // min(masks) for m in masks))
        if r + 1 < ROUNDS and not moves[r] and not (two and r == 1):
            extra, more = sums(r + 1)
            ins.update(next_index=sets[r + 1][0], next_tiles=sets[r + 1][1], **extra)
            outs.update(more)
        out = call(kernel, ins, outs, scratch + (scratch_sum if "sent" in outs else []))
        held = out["held"]
        if two and r < 2:
            for later in range(r + 2, ROUNDS, 2):
                known[later] = out["counts"] if r == 1 else shift(out["counts"])
        if r + 1 < ROUNDS and "sent" not in out:
            if moves[r]:
                held = shift(held)
                if two:
                    held, far_index, far_tiles[0] = lax.optimization_barrier((held, far_index, far_tiles[0]))
            out = project(held, r + 1)
    return joined(core, held[0], swap_cores(held[1]))


def solution(mesh):
    in_specs = (
        P("subset", "tile"),
        P("subset", "tile", None, None),
        P("subset", "tile"),
        P("subset", "tile"),
        P("subset", "tile"),
        P("subset", None, "tile"),
    )
    return jax.shard_map(shards, mesh=mesh, in_specs=in_specs, out_specs=P("subset", "tile"),
                         check_vma=False)
```

```python
import functools

import jax
import jax.numpy as jnp
from jax import lax
from jax.experimental import pallas as pl
from jax.experimental.pallas import tpu as pltpu
from jax.sharding import PartitionSpec as P

TILE_GROUP = 32
ROUNDS = 4
CORES = 2
LANES = 128
VMEM_LIMIT = 40 * 1024 * 1024


def each_live(index_ref, slots, body):
    live = index_ref[2, 0]
    for group in range(-(-slots // TILE_GROUP)):
        first, last = group * TILE_GROUP, min(slots, (group + 1) * TILE_GROUP)

        @pl.when(group < live)
        def _():
            for t in range(first, last, 2):
                body(tuple(range(t, min(t + 2, last))))


def add_products(acc, left_of, targets, wide, transposed):
    left = jnp.concatenate(left_of, axis=0)
    dims = (((1,), (1,)), ((), ())) if transposed else (((1,), (0,)), ((), ()))
    part = lax.dot_general(left, wide, dims, preferred_element_type=jnp.float32)
    rows, size = acc.shape[1:]
    for i, at in enumerate(targets):
        used = part[i * left_of[i].shape[0]:, i * size:(i + 1) * size][:rows]
        acc[at] = acc[at] + used


def tile_at(tile_refs, t):
    for ref in tile_refs:
        if t < ref.shape[0]:
            return ref[t]
        t -= ref.shape[0]


def slots_of(tile_refs):
    return sum(ref.shape[0] for ref in tile_refs)


def project_into(acc, low, index_refs, sets):
    blocks = low.shape[0] // CORES
    for k in range(CORES):
        if sets[k] is None:
            continue
        index_ref, tile_refs = index_refs[k], sets[k]

        def body(ts):
            wide = jnp.concatenate([tile_at(tile_refs, t) for t in ts], axis=0)
            add_products(acc, [low[k * blocks + index_ref[0, t]] for t in ts],
                         [index_ref[1, t] for t in ts], wide, True)

        each_live(index_ref, slots_of(tile_refs), body)


def back_into(acc, ratios, index_refs, sets):
    blocks = acc.shape[0] // CORES
    acc[...] = jnp.zeros_like(acc)
    for k in range(CORES):
        index_ref, tile_refs = index_refs[k], sets[k]

        def body(ts):
            wide = jnp.concatenate([tile_at(tile_refs, t) for t in ts], axis=1)
            add_products(acc, [ratios(index_ref[1, t]) for t in ts],
                         [k * blocks + index_ref[0, t] for t in ts], wide, False)

        each_live(index_ref, slots_of(tile_refs), body)


def columns(blocks, size):
    for k in range(CORES):
        for b in range(blocks):
            yield k, slice(b * size, (b + 1) * size), k * blocks + b


def piece_of(held, k, cols):
    return held[k][:, cols] if isinstance(held, tuple) else held[k, :, cols]


def write_sums(ins, outs, acc):
    blocks = acc.shape[0]
    outs["wide"][...] = acc[...]
    outs["sent"][:blocks] = acc[...].astype(jnp.bfloat16)
    if "dealt" in ins:
        outs["sent"][blocks:] = ins["dealt"][...]


def first_kernel(ins, outs, low, acc, own, arrived):
    copy = pltpu.make_async_copy(ins["own_hbm"], own, arrived)
    copy.start()
    blocks, size = low.shape[0] // CORES, low.shape[-1]
    for k, cols, at in columns(blocks, size):
        low[at] = piece_of(ins["held"], k, cols).astype(jnp.bfloat16)
    acc[...] = jnp.zeros_like(acc)
    project_into(acc, low, ins["index"], (None, ins["tiles"]))
    copy.wait()
    project_into(acc, low, ins["index"], ((own,), None))
    write_sums(ins, outs, acc)


def project_kernel(ins, outs, low, acc):
    blocks, size = low.shape[0] // CORES, low.shape[-1]
    acc[...] = jnp.zeros_like(acc)
    for k, cols, at in columns(blocks, size):
        low[at] = piece_of(ins["held"], k, cols).astype(jnp.bfloat16)
    project_into(acc, low, ins["index"], ins["tiles"])
    write_sums(ins, outs, acc)


def sensitivity_kernel(ins, outs, acc):
    ones = jnp.ones((16, ins["tiles"][0][0].shape[1]), jnp.bfloat16)
    back_into(acc, lambda ray: ones, ins["index"], ins["tiles"])
    outs["inverse"][...] = 1.0 / acc[...]


def update_kernel(masks, ins, outs, counts, ratios, back, *scratch):
    blocks, size = back.shape[0] // CORES, back.shape[-1]
    rays = ratios.shape[0]
    total = ins["wide"][...]
    for got in ins["got"]:
        total = total + got[:rays].astype(jnp.float32)
    if "counts" in ins:
        counts[...] = ins["counts"][...]
    else:
        place = ins["index"][0][3, 0]
        share = ins["sent"].shape[0] - rays
        for mask, part in zip((0,) + masks, (ins["sent"],) + tuple(ins["got"])):
            counts[pl.ds((place ^ mask) * share, share)] = part[rays:]
    if "counts" in outs:
        outs["counts"][...] = counts[...]
    ratios[...] = (counts[...].astype(jnp.float32) / total).astype(jnp.bfloat16)
    back_into(back, lambda ray: ratios[ray], ins["index"], ins["tiles"])
    for k, cols, at in columns(blocks, size):
        value = piece_of(ins["held"], k, cols) * back[at] * ins["inverse"][at, :1]
        outs["held"][k, :, cols] = value
        if "sent" in outs:
            scratch[0][at] = value.astype(jnp.bfloat16)
    if "sent" in outs:
        scratch[1][...] = jnp.zeros_like(scratch[1])
        project_into(scratch[1], scratch[0], ins["next_index"], ins["next_tiles"])
        write_sums(ins, outs, scratch[1])


def call(kernel, ins, outs, scratch):
    def spec(path, _):
        name = path[0].key
        space = pltpu.SMEM if name.endswith("index") else pltpu.HBM if name.endswith("hbm") else pltpu.VMEM
        return pl.BlockSpec(memory_space=space)

    return pl.pallas_call(
        kernel,
        out_shape=outs,
        in_specs=[jax.tree_util.tree_map_with_path(spec, ins)],
        out_specs=jax.tree_util.tree_map_with_path(spec, outs),
        scratch_shapes=scratch,
        compiler_params=pltpu.CompilerParams(vmem_limit_bytes=VMEM_LIMIT))(ins)


def shards(images, system_tiles, tile_vox, tile_ray, live_blocks, counts):
    frames, voxels = images.shape
    half = frames // CORES
    size = system_tiles.shape[-1]
    vox_blocks = voxels // size
    own_tiles = system_tiles[0]
    slots = own_tiles.shape[0]
    tile_devs = lax.axis_size("tile")
    chips = tile_devs // CORES
    rb_dev = counts.shape[2] // size
    ray_blocks = rb_dev * tile_devs
    subset_count = lax.axis_size("subset")
    position = lax.axis_index("subset")
    core = lax.axis_index("tile") % CORES
    chip = lax.axis_index("tile") // CORES
    both = CORES * vox_blocks
    f32, bf16 = jnp.float32, jnp.bfloat16
    shaped = jax.ShapeDtypeStruct

    steps, bit = [], 1
    while bit < chips:
        wide_step = bit * 4 <= chips
        steps.append((bit, 2 * bit, 3 * bit) if wide_step else (bit,))
        bit *= 4 if wide_step else 2

    def place(masks):
        return chip // min(masks) % (len(masks) + 1)

    def swap_cores(array):
        return lax.ppermute(array, "tile", [(i, i ^ 1) for i in range(tile_devs)])

    def swap_chips(array, mask):
        pairs = [(CORES * j + c, CORES * (j ^ mask) + c) for j in range(chips) for c in range(CORES)]
        return lax.ppermute(array, "tile", pairs)

    def joined(side, own, other):
        return jnp.where(side == 0, jnp.concatenate([own, other]), jnp.concatenate([other, own]))

    def shift(array):
        return lax.ppermute(array, "subset", [(i, (i + 1) % subset_count) for i in range(subset_count)])

    def after(array, value):
        return lax.optimization_barrier((array, value))[0]

    halves = images.reshape(CORES, half, voxels)
    mine = lax.dynamic_index_in_dim(halves, core, 0, keepdims=False)
    theirs = lax.dynamic_index_in_dim(halves, 1 - core, 0, keepdims=False)
    rows = jnp.concatenate([tile_vox, tile_ray, jnp.broadcast_to(live_blocks, tile_vox.shape),
                            jnp.broadcast_to(place(steps[-1]), tile_vox.shape)], axis=0)
    own_index = jnp.pad(rows, ((0, 4), (0, -slots % LANES)))
    tiles = ((own_tiles,), (swap_cores(own_tiles),))
    held = (mine, swap_cores(theirs))
    index = (own_index, swap_cores(own_index))

    dealt = counts[0].astype(bf16).reshape(subset_count, CORES, half, rb_dev, size).transpose(1, 3, 0, 2, 4)
    kept = lax.dynamic_index_in_dim(dealt, core, 0, keepdims=False)
    got = swap_cores(lax.dynamic_index_in_dim(dealt, 1 - core, 0, keepdims=False))
    dealt = joined(core, kept, got)

    def dealt_of(panel):
        return lax.dynamic_index_in_dim(dealt, panel % subset_count, 1, keepdims=False)

    def sensitivity(index, tiles):
        return call(sensitivity_kernel, {"index": index, "tiles": tiles},
                    {"inverse": shaped((both, 8, size), f32)},
                    [pltpu.VMEM((both, 8, size), f32)])["inverse"]

    sets = [(index, tiles, sensitivity(index, tiles))] * ROUNDS
    moves = [True] * (ROUNDS - 1)
    known = [None] * ROUNDS
    two = subset_count == 2
    if two:
        moves = [r == 0 for r in range(ROUNDS - 1)]

    scratch_sum = [pltpu.VMEM((both, half, size), bf16), pltpu.VMEM((ray_blocks, half, size), f32)]
    scratch = [pltpu.VMEM((ray_blocks, half, size), bf16)] * 2 + [pltpu.VMEM((both, half, size), f32)]

    def sums(r):
        fresh = known[r] is None
        sent = ray_blocks + fresh * rb_dev * CORES
        return ({"dealt": dealt_of(position - r)} if fresh else {},
                {"wide": shaped((ray_blocks, half, size), f32), "sent": shaped((sent, half, size), bf16)})

    def project(held, r):
        extra, outs = sums(r)
        return call(project_kernel, {"held": held, "index": sets[r][0], "tiles": sets[r][1], **extra},
                    outs, scratch_sum)

    extra, outs = sums(0)
    out = call(first_kernel, {"held": held, "index": index, "own_hbm": own_tiles, "tiles": tiles[1], **extra},
               outs, scratch_sum + [pltpu.VMEM(own_tiles.shape, bf16), pltpu.SemaphoreType.DMA])
    for r in range(ROUNDS):
        wide, sent = out["wide"], out["sent"]
        if two and r == 0:
            far_index = shift(after(own_index, sent))
            far_tiles = [shift(after(own_tiles[:slots * 5 // 8], sent))]
        if two and r == 1:
            far_index = (far_index, swap_cores(after(far_index, sent)))
            far_swapped = [swap_cores(after(far_tiles[0], sent))]
            far_tiles.append(shift(after(own_tiles[slots * 5 // 8:], sent)))
        for masks in steps:
            got = [swap_chips(sent, mask) for mask in masks]
            if masks is not steps[-1]:
                wide = wide + sum(part[:ray_blocks].astype(f32) for part in got)
                own, counted = place(masks), wide.astype(bf16)
                if sent.shape[0] > ray_blocks:
                    parts = dict(zip((0,) + masks, [sent] + got))
                    ordered = [parts[m * min(masks)][ray_blocks:] for m in range(len(parts))]
                    if len(ordered) == 2:
                        passed = joined(own, *ordered)
                    else:
                        passed = jnp.concatenate([lax.dynamic_index_in_dim(
                            jnp.stack(ordered), own ^ v, 0, keepdims=False) for v in range(len(ordered))])
                    counted = jnp.concatenate([counted, passed])
                sent = counted
        if two and r == 1:
            far_swapped.append(swap_cores(after(far_tiles[1], tuple(got))))
            far_tiles = (tuple(far_tiles), tuple(far_swapped))
            far = (far_index, far_tiles, sensitivity(far_index, far_tiles))
            sets = [far if later >= 2 and later % 2 == 0 else sets[later] for later in range(ROUNDS)]
        ins = {"wide": wide, "got": got, "held": held,
               "index": sets[r][0], "tiles": sets[r][1], "inverse": sets[r][2]}
        outs = {"held": shaped((CORES, half, voxels), f32)}
        if known[r] is None:
            ins["sent"] = sent
            if two:
                outs["counts"] = shaped((ray_blocks, half, size), bf16)
        else:
            ins["counts"] = known[r]
        kernel = functools.partial(update_kernel, tuple(m // min(masks) for m in masks))
        if r + 1 < ROUNDS and not moves[r] and not (two and r == 1):
            extra, more = sums(r + 1)
            ins.update(next_index=sets[r + 1][0], next_tiles=sets[r + 1][1], **extra)
            outs.update(more)
        out = call(kernel, ins, outs, scratch + (scratch_sum if "sent" in outs else []))
        held = out["held"]
        if two and r < 2:
            for later in range(r + 2, ROUNDS, 2):
                known[later] = out["counts"] if r == 1 else shift(out["counts"])
        if r + 1 < ROUNDS and "sent" not in out:
            if moves[r]:
                held = shift(held)
                if two:
                    held, far_index, far_tiles[0] = lax.optimization_barrier((held, far_index, far_tiles[0]))
            out = project(held, r + 1)
    return joined(core, held[0], swap_cores(held[1]))


def solution(mesh):
    in_specs = (
        P("subset", "tile"),
        P("subset", "tile", None, None),
        P("subset", "tile"),
        P("subset", "tile"),
        P("subset", "tile"),
        P("subset", None, "tile"),
    )
    return jax.shard_map(shards, mesh=mesh, in_specs=in_specs, out_specs=P("subset", "tile"),
                         check_vma=False)
```

```python
import functools

import jax
import jax.numpy as jnp
from jax import lax
from jax.experimental import pallas as pl
from jax.experimental.pallas import tpu as pltpu
from jax.sharding import PartitionSpec as P

TILE_GROUP = 32
ROUNDS = 4
CORES = 2
LANES = 128
VMEM_LIMIT = 40 * 1024 * 1024


def each_live(index_ref, slots, body):
    live = index_ref[2, 0]
    for group in range(-(-slots // TILE_GROUP)):
        first, last = group * TILE_GROUP, min(slots, (group + 1) * TILE_GROUP)

        @pl.when(group < live)
        def _():
            for t in range(first, last, 2):
                body(tuple(range(t, min(t + 2, last))))


def add_products(acc, left_of, targets, wide, transposed):
    left = jnp.concatenate(left_of, axis=0)
    dims = (((1,), (1,)), ((), ())) if transposed else (((1,), (0,)), ((), ()))
    part = lax.dot_general(left, wide, dims, preferred_element_type=jnp.float32)
    rows, size = acc.shape[1:]
    for i, at in enumerate(targets):
        used = part[i * left_of[i].shape[0]:, i * size:(i + 1) * size][:rows]
        acc[at] = acc[at] + used


def tile_at(tile_refs, t):
    for ref in tile_refs:
        if t < ref.shape[0]:
            return ref[t]
        t -= ref.shape[0]


def slots_of(tile_refs):
    return sum(ref.shape[0] for ref in tile_refs)


def project_into(acc, low, index_refs, sets):
    blocks = low.shape[0] // CORES
    for k in range(CORES):
        if sets[k] is None:
            continue
        index_ref, tile_refs = index_refs[k], sets[k]

        def body(ts):
            wide = jnp.concatenate([tile_at(tile_refs, t) for t in ts], axis=0)
            add_products(acc, [low[k * blocks + index_ref[0, t]] for t in ts],
                         [index_ref[1, t] for t in ts], wide, True)

        each_live(index_ref, slots_of(tile_refs), body)


def back_into(acc, ratios, index_refs, sets):
    blocks = acc.shape[0] // CORES
    acc[...] = jnp.zeros_like(acc)
    for k in range(CORES):
        if sets[k] is None:
            continue
        index_ref, tile_refs = index_refs[k], sets[k]

        def body(ts):
            wide = jnp.concatenate([tile_at(tile_refs, t) for t in ts], axis=1)
            add_products(acc, [ratios(index_ref[1, t]) for t in ts],
                         [k * blocks + index_ref[0, t] for t in ts], wide, False)

        each_live(index_ref, slots_of(tile_refs), body)


def columns(held, size):
    for k in range(CORES):
        if held[k] is not None:
            blocks = held[k].shape[1] // size
            for b in range(blocks):
                yield k, slice(b * size, (b + 1) * size), k * blocks + b


def write_sums(ins, outs, acc):
    blocks = acc.shape[0]
    outs["wide"][...] = acc[...]
    if "sent" in outs:
        outs["sent"][:blocks] = acc[...].astype(jnp.bfloat16)
        if "dealt" in ins:
            outs["sent"][blocks:] = ins["dealt"][...]


def first_kernel(ins, outs, low, acc, own, arrived):
    copy = pltpu.make_async_copy(ins["own_hbm"], own, arrived)
    copy.start()
    for k, cols, at in columns(ins["held"], low.shape[-1]):
        low[at] = ins["held"][k][:, cols].astype(jnp.bfloat16)
    acc[...] = jnp.zeros_like(acc)
    project_into(acc, low, ins["index"], (None, ins["tiles"]))
    copy.wait()
    project_into(acc, low, ins["index"], ((own,), None))
    write_sums(ins, outs, acc)


def project_kernel(ins, outs, low, acc):
    acc[...] = ins["begun"][...] if "begun" in ins else jnp.zeros_like(acc)
    for k, cols, at in columns(ins["held"], low.shape[-1]):
        low[at] = ins["held"][k][:, cols].astype(jnp.bfloat16)
    project_into(acc, low, ins["index"], ins["tiles"])
    write_sums(ins, outs, acc)


def sensitivity_kernel(ins, outs, acc):
    ones = jnp.ones((16, ins["tiles"][0][0].shape[1]), jnp.bfloat16)
    back_into(acc, lambda ray: ones, ins["index"], ins["tiles"])
    outs["inverse"][...] = 1.0 / acc[...]


def form_ratios(masks, ins, outs, counts, ratios):
    rays = ratios.shape[0]
    total = ins["wide"][...]
    for got in ins["got"]:
        total = total + got[:rays].astype(jnp.float32)
    if "counts" in ins:
        counts[...] = ins["counts"][...]
    else:
        place = ins["index"][0][3, 0]
        share = ins["sent"].shape[0] - rays
        for mask, part in zip((0,) + masks, (ins["sent"],) + tuple(ins["got"])):
            counts[pl.ds((place ^ mask) * share, share)] = part[rays:]
    if "counts" in outs:
        outs["counts"][...] = counts[...]
    ratios[...] = (counts[...].astype(jnp.float32) / total).astype(jnp.bfloat16)
    if "ratios" in outs:
        outs["ratios"][...] = ratios[...]


def update_kernel(masks, ins, outs, back, *scratch):
    if "ratios" in ins:
        ratios = ins["ratios"]
    else:
        counts, ratios, *scratch = scratch
        form_ratios(masks, ins, outs, counts, ratios)
    back_into(back, lambda ray: ratios[ray], ins["index"], ins["tiles"])
    for k, cols, at in columns(ins["held"], back.shape[-1]):
        value = ins["held"][k][:, cols] * back[at] * ins["inverse"][at, :1]
        outs["held"][k][:, cols] = value
        if "sent" in outs:
            scratch[0][at] = value.astype(jnp.bfloat16)
    if "sent" in outs:
        scratch[1][...] = jnp.zeros_like(scratch[1])
        project_into(scratch[1], scratch[0], ins["next_index"], ins["next_tiles"])
        write_sums(ins, outs, scratch[1])


def call(kernel, ins, outs, scratch):
    def spec(path, _):
        name = path[0].key
        space = pltpu.SMEM if name.endswith("index") else pltpu.HBM if name.endswith("hbm") else pltpu.VMEM
        return pl.BlockSpec(memory_space=space)

    return pl.pallas_call(
        kernel,
        out_shape=outs,
        in_specs=[jax.tree_util.tree_map_with_path(spec, ins)],
        out_specs=jax.tree_util.tree_map_with_path(spec, outs),
        scratch_shapes=scratch,
        compiler_params=pltpu.CompilerParams(vmem_limit_bytes=VMEM_LIMIT))(ins)


def shards(images, system_tiles, tile_vox, tile_ray, live_blocks, counts):
    frames, voxels = images.shape
    half = frames // CORES
    size = system_tiles.shape[-1]
    vox_blocks = voxels // size
    own_tiles = system_tiles[0]
    slots = own_tiles.shape[0]
    tile_devs = lax.axis_size("tile")
    chips = tile_devs // CORES
    rb_dev = counts.shape[2] // size
    ray_blocks = rb_dev * tile_devs
    subset_count = lax.axis_size("subset")
    position = lax.axis_index("subset")
    core = lax.axis_index("tile") % CORES
    chip = lax.axis_index("tile") // CORES
    both = CORES * vox_blocks
    f32, bf16 = jnp.float32, jnp.bfloat16
    shaped = jax.ShapeDtypeStruct

    steps, bit = [], 1
    while bit < chips:
        wide_step = bit * 4 <= chips
        steps.append((bit, 2 * bit, 3 * bit) if wide_step else (bit,))
        bit *= 4 if wide_step else 2

    def place(masks):
        return chip // min(masks) % (len(masks) + 1)

    def swap_cores(array):
        return lax.ppermute(array, "tile", [(i, i ^ 1) for i in range(tile_devs)])

    def swap_chips(array, mask):
        pairs = [(CORES * j + c, CORES * (j ^ mask) + c) for j in range(chips) for c in range(CORES)]
        return lax.ppermute(array, "tile", pairs)

    def joined(side, own, other):
        return jnp.where(side == 0, jnp.concatenate([own, other]), jnp.concatenate([other, own]))

    def shift(array):
        return lax.ppermute(array, "subset", [(i, (i + 1) % subset_count) for i in range(subset_count)])

    def after(array, value):
        return lax.optimization_barrier((array, value))[0]

    halves = images.reshape(CORES, half, voxels)
    mine = lax.dynamic_index_in_dim(halves, core, 0, keepdims=False)
    theirs = lax.dynamic_index_in_dim(halves, 1 - core, 0, keepdims=False)
    rows = jnp.concatenate([tile_vox, tile_ray, jnp.broadcast_to(live_blocks, tile_vox.shape),
                            jnp.broadcast_to(place(steps[-1]), tile_vox.shape)], axis=0)
    own_index = jnp.pad(rows, ((0, 4), (0, -slots % LANES)))
    tiles = ((own_tiles,), (swap_cores(own_tiles),))
    held = (mine, swap_cores(theirs))
    index = (own_index, swap_cores(own_index))

    dealt = counts[0].astype(bf16).reshape(subset_count, CORES, half, rb_dev, size).transpose(1, 3, 0, 2, 4)
    kept = lax.dynamic_index_in_dim(dealt, core, 0, keepdims=False)
    got = swap_cores(lax.dynamic_index_in_dim(dealt, 1 - core, 0, keepdims=False))
    dealt = joined(core, kept, got)

    def dealt_of(panel):
        return lax.dynamic_index_in_dim(dealt, panel % subset_count, 1, keepdims=False)

    def sensitivity(index, tiles):
        return call(sensitivity_kernel, {"index": index, "tiles": tiles},
                    {"inverse": shaped((both, 8, size), f32)},
                    [pltpu.VMEM((both, 8, size), f32)])["inverse"]

    sets = [(index, tiles, sensitivity(index, tiles))] * ROUNDS
    moves = [True] * (ROUNDS - 1)
    known = [None] * ROUNDS
    two = subset_count == 2
    if two:
        far_tiles = shift(after(own_tiles, (theirs, own_index)))
    if two:
        moves = [r == 0 for r in range(ROUNDS - 1)]

    low_scratch, back_scratch = pltpu.VMEM((both, half, size), bf16), pltpu.VMEM((both, half, size), f32)
    ray_scratch, sum_scratch = (pltpu.VMEM((ray_blocks, half, size), kind) for kind in (bf16, f32))
    piece = shaped((half, voxels), f32)
    summed = shaped((ray_blocks, half, size), f32)

    def only(k, pair):
        return tuple(value if i == k else None for i, value in enumerate(pair))

    def sums(r):
        fresh = known[r] is None
        sent = ray_blocks + fresh * rb_dev * CORES
        return ({"dealt": dealt_of(position - r)} if fresh else {},
                {"wide": summed, "sent": shaped((sent, half, size), bf16)})

    extra, outs = sums(0)
    out = call(first_kernel, {"held": held, "index": index, "own_hbm": own_tiles, "tiles": tiles[1], **extra},
               outs, [low_scratch, sum_scratch, pltpu.VMEM(own_tiles.shape, bf16), pltpu.SemaphoreType.DMA])
    for r in range(ROUNDS):
        wide, sent = out["wide"], out["sent"]
        if two and r == 0:
            far_index = shift(after(own_index, sent))
        if two and r == 1:
            far_index = (far_index, swap_cores(after(far_index, sent)))
            far_tiles = ((far_tiles,), (swap_cores(after(far_tiles, sent)),))
            far = (far_index, far_tiles, sensitivity(far_index, far_tiles))
            sets = [far if later >= 2 and later % 2 == 0 else sets[later] for later in range(ROUNDS)]
        for masks in steps:
            got = [swap_chips(sent, mask) for mask in masks]
            if masks is not steps[-1]:
                wide = wide + sum(part[:ray_blocks].astype(f32) for part in got)
                own, counted = place(masks), wide.astype(bf16)
                if sent.shape[0] > ray_blocks:
                    parts = dict(zip((0,) + masks, [sent] + got))
                    ordered = [parts[m * min(masks)][ray_blocks:] for m in range(len(parts))]
                    if len(ordered) == 2:
                        passed = joined(own, *ordered)
                    else:
                        passed = jnp.concatenate([lax.dynamic_index_in_dim(
                            jnp.stack(ordered), own ^ v, 0, keepdims=False) for v in range(len(ordered))])
                    counted = jnp.concatenate([counted, passed])
                sent = counted
        if two and r == 0:
            wide, far_index = lax.optimization_barrier((wide, far_index))
        now_index, now_tiles, now_inverse = sets[r]
        base = {"index": now_index, "inverse": now_inverse}
        ins = {"wide": wide, "got": got, **base}
        outs = {}
        if known[r] is None:
            ins["sent"] = sent
            if two:
                outs["counts"] = summed.update(dtype=bf16)
        else:
            ins["counts"] = known[r]
        kernel = functools.partial(update_kernel, tuple(m // min(masks) for m in masks))
        last = r + 1 == ROUNDS
        if last or moves[r]:
            order = (1, 0) if last else (0, 1)
            moved, ratios = {}, None
            for k in order:
                if ratios is None:
                    out = call(kernel, {**ins, "held": only(k, held), "tiles": only(k, now_tiles)},
                               {"held": only(k, (piece,) * CORES), "ratios": summed.update(dtype=bf16), **outs},
                               [back_scratch, ray_scratch, ray_scratch])
                    ratios = out["ratios"]
                    if two and r == 0:
                        far_counts = shift(out["counts"])
                else:
                    out = {**out, **call(kernel, {**base, "ratios": ratios, "held": only(k, held),
                                                  "tiles": only(k, now_tiles)},
                                         {"held": only(k, (piece,) * CORES)}, [back_scratch])}
                moved[k] = out["held"][k]
                if not last:
                    moved[k] = shift(moved[k])
                elif k == 1:
                    moved[k] = swap_cores(moved[k])
            held = (moved[0], moved[1])
            if not last:
                extra, more = sums(r + 1)
                begun = call(project_kernel, {"held": only(0, held), "index": sets[r + 1][0],
                                              "tiles": only(0, sets[r + 1][1])},
                             {"wide": summed}, [low_scratch, sum_scratch])["wide"]
                out = call(project_kernel, {"held": only(1, held), "index": sets[r + 1][0], "begun": begun,
                                            "tiles": only(1, sets[r + 1][1]), **extra},
                           more, [low_scratch, sum_scratch])
        else:
            if two and r == 1:
                known[r + 1] = far_counts
            extra, more = sums(r + 1)
            ins.update(held=held, tiles=now_tiles, next_index=sets[r + 1][0], next_tiles=sets[r + 1][1], **extra)
            outs.update(held=(piece,) * CORES, **more)
            out = call(kernel, ins, outs, [back_scratch, ray_scratch, ray_scratch, low_scratch, sum_scratch])
            held = out["held"]
            if two and r == 1:
                known = [known[later] if later < 2 else far_counts if later % 2 == 0 else out["counts"]
                         for later in range(ROUNDS)]
    return joined(core, held[0], held[1])


def solution(mesh):
    in_specs = (
        P("subset", "tile"),
        P("subset", "tile", None, None),
        P("subset", "tile"),
        P("subset", "tile"),
        P("subset", "tile"),
        P("subset", None, "tile"),
    )
    return jax.shard_map(shards, mesh=mesh, in_specs=in_specs, out_specs=P("subset", "tile"),
                         check_vma=False)
```

```python
import functools

import jax
import jax.numpy as jnp
from jax import lax
from jax.experimental import pallas as pl
from jax.experimental.pallas import tpu as pltpu
from jax.sharding import PartitionSpec as P

TILE_GROUP = 32
ROUNDS = 4
CORES = 2
LANES = 128
VMEM_LIMIT = 40 * 1024 * 1024


def each_live(index_ref, slots, body):
    live = index_ref[2, 0]
    for group in range(-(-slots // TILE_GROUP)):
        first, last = group * TILE_GROUP, min(slots, (group + 1) * TILE_GROUP)

        @pl.when(group < live)
        def _():
            for t in range(first, last, 2):
                body(tuple(range(t, min(t + 2, last))))


def add_products(acc, left_of, targets, wide, transposed):
    left = jnp.concatenate(left_of, axis=0)
    dims = (((1,), (1,)), ((), ())) if transposed else (((1,), (0,)), ((), ()))
    part = lax.dot_general(left, wide, dims, preferred_element_type=jnp.float32)
    rows, size = acc.shape[1:]
    for i, at in enumerate(targets):
        used = part[i * left_of[i].shape[0]:, i * size:(i + 1) * size][:rows]
        acc[at] = acc[at] + used


def tile_at(tile_refs, t):
    for ref in tile_refs:
        if t < ref.shape[0]:
            return ref[t]
        t -= ref.shape[0]


def slots_of(tile_refs):
    return sum(ref.shape[0] for ref in tile_refs)


def project_into(acc, low, index_refs, sets):
    blocks = low.shape[0] // CORES
    for k in range(CORES):
        if sets[k] is None:
            continue
        index_ref, tile_refs = index_refs[k], sets[k]

        def body(ts):
            wide = jnp.concatenate([tile_at(tile_refs, t) for t in ts], axis=0)
            add_products(acc, [low[k * blocks + index_ref[0, t]] for t in ts],
                         [index_ref[1, t] for t in ts], wide, True)

        each_live(index_ref, slots_of(tile_refs), body)


def back_into(acc, ratios, index_refs, sets):
    blocks = acc.shape[0] // CORES
    acc[...] = jnp.zeros_like(acc)
    for k in range(CORES):
        if sets[k] is None:
            continue
        index_ref, tile_refs = index_refs[k], sets[k]

        def body(ts):
            wide = jnp.concatenate([tile_at(tile_refs, t) for t in ts], axis=1)
            add_products(acc, [ratios(index_ref[1, t]) for t in ts],
                         [k * blocks + index_ref[0, t] for t in ts], wide, False)

        each_live(index_ref, slots_of(tile_refs), body)


def columns(held, size):
    for k in range(CORES):
        if held[k] is not None:
            blocks = held[k].shape[1] // size
            for b in range(blocks):
                yield k, slice(b * size, (b + 1) * size), k * blocks + b


def write_sums(ins, outs, acc):
    blocks = acc.shape[0]
    outs["wide"][...] = acc[...]
    if "sent" in outs:
        outs["sent"][:blocks] = acc[...].astype(jnp.bfloat16)
        if "dealt" in ins:
            outs["sent"][blocks:] = ins["dealt"][...]


def first_kernel(ins, outs, low, acc, own, arrived):
    copy = pltpu.make_async_copy(ins["own_hbm"], own, arrived)
    copy.start()
    for k, cols, at in columns(ins["held"], low.shape[-1]):
        low[at] = ins["held"][k][:, cols].astype(jnp.bfloat16)
    acc[...] = jnp.zeros_like(acc)
    project_into(acc, low, ins["index"], (None, ins["tiles"]))
    copy.wait()
    project_into(acc, low, ins["index"], ((own,), None))
    write_sums(ins, outs, acc)


def project_kernel(ins, outs, low, acc):
    acc[...] = ins["begun"][...] if "begun" in ins else jnp.zeros_like(acc)
    for k, cols, at in columns(ins["held"], low.shape[-1]):
        low[at] = ins["held"][k][:, cols].astype(jnp.bfloat16)
    project_into(acc, low, ins["index"], ins["tiles"])
    write_sums(ins, outs, acc)


def sensitivity_kernel(ins, outs, acc):
    ones = jnp.ones((16, ins["tiles"][0][0].shape[1]), jnp.bfloat16)
    back_into(acc, lambda ray: ones, ins["index"], ins["tiles"])
    outs["inverse"][...] = 1.0 / acc[...]


def form_ratios(masks, ins, outs, counts, ratios):
    rays = ratios.shape[0]
    total = ins["wide"][...]
    for got in ins["got"]:
        total = total + got[:rays].astype(jnp.float32)
    if "counts" in ins:
        counts[...] = ins["counts"][...]
    else:
        place = ins["index"][0][3, 0]
        share = ins["sent"].shape[0] - rays
        for mask, part in zip((0,) + masks, (ins["sent"],) + tuple(ins["got"])):
            counts[pl.ds((place ^ mask) * share, share)] = part[rays:]
    if "counts" in outs:
        outs["counts"][...] = counts[...]
    ratios[...] = (counts[...].astype(jnp.float32) / total).astype(jnp.bfloat16)
    if "ratios" in outs:
        outs["ratios"][...] = ratios[...]


def update_kernel(masks, ins, outs, back, *scratch):
    if "ratios" in ins:
        ratios = ins["ratios"]
    else:
        counts, ratios, *scratch = scratch
        form_ratios(masks, ins, outs, counts, ratios)
    back_into(back, lambda ray: ratios[ray], ins["index"], ins["tiles"])
    for k, cols, at in columns(ins["held"], back.shape[-1]):
        value = ins["held"][k][:, cols] * back[at] * ins["inverse"][at, :1]
        outs["held"][k][:, cols] = value
        if "sent" in outs:
            scratch[0][at] = value.astype(jnp.bfloat16)
    if "sent" in outs:
        scratch[1][...] = jnp.zeros_like(scratch[1])
        project_into(scratch[1], scratch[0], ins["next_index"], ins["next_tiles"])
        write_sums(ins, outs, scratch[1])


def call(kernel, ins, outs, scratch):
    def spec(path, _):
        name = path[0].key
        space = pltpu.SMEM if name.endswith("index") else pltpu.HBM if name.endswith("hbm") else pltpu.VMEM
        return pl.BlockSpec(memory_space=space)

    return pl.pallas_call(
        kernel,
        out_shape=outs,
        in_specs=[jax.tree_util.tree_map_with_path(spec, ins)],
        out_specs=jax.tree_util.tree_map_with_path(spec, outs),
        scratch_shapes=scratch,
        compiler_params=pltpu.CompilerParams(vmem_limit_bytes=VMEM_LIMIT))(ins)


def shards(images, system_tiles, tile_vox, tile_ray, live_blocks, counts):
    frames, voxels = images.shape
    half = frames // CORES
    size = system_tiles.shape[-1]
    vox_blocks = voxels // size
    own_tiles = system_tiles[0]
    slots = own_tiles.shape[0]
    tile_devs = lax.axis_size("tile")
    chips = tile_devs // CORES
    rb_dev = counts.shape[2] // size
    ray_blocks = rb_dev * tile_devs
    subset_count = lax.axis_size("subset")
    position = lax.axis_index("subset")
    core = lax.axis_index("tile") % CORES
    chip = lax.axis_index("tile") // CORES
    both = CORES * vox_blocks
    f32, bf16 = jnp.float32, jnp.bfloat16
    shaped = jax.ShapeDtypeStruct

    steps, bit = [], 1
    while bit < chips:
        wide_step = bit * 4 <= chips
        steps.append((bit, 2 * bit, 3 * bit) if wide_step else (bit,))
        bit *= 4 if wide_step else 2

    def place(masks):
        return chip // min(masks) % (len(masks) + 1)

    def swap_cores(array):
        return lax.ppermute(array, "tile", [(i, i ^ 1) for i in range(tile_devs)])

    def swap_chips(array, mask):
        pairs = [(CORES * j + c, CORES * (j ^ mask) + c) for j in range(chips) for c in range(CORES)]
        return lax.ppermute(array, "tile", pairs)

    def joined(side, own, other):
        return jnp.where(side == 0, jnp.concatenate([own, other]), jnp.concatenate([other, own]))

    def shift(array):
        return lax.ppermute(array, "subset", [(i, (i + 1) % subset_count) for i in range(subset_count)])

    def after(array, value):
        return lax.optimization_barrier((array, value))[0]

    halves = images.reshape(CORES, half, voxels)
    mine = lax.dynamic_index_in_dim(halves, core, 0, keepdims=False)
    theirs = lax.dynamic_index_in_dim(halves, 1 - core, 0, keepdims=False)
    rows = jnp.concatenate([tile_vox, tile_ray, jnp.broadcast_to(live_blocks, tile_vox.shape),
                            jnp.broadcast_to(place(steps[-1]), tile_vox.shape)], axis=0)
    own_index = jnp.pad(rows, ((0, 4), (0, -slots % LANES)))
    tiles = ((own_tiles,), (swap_cores(own_tiles),))
    held = (mine, swap_cores(theirs))
    index = (own_index, swap_cores(own_index))

    dealt = counts[0].astype(bf16).reshape(subset_count, CORES, half, rb_dev, size).transpose(1, 3, 0, 2, 4)
    kept = lax.dynamic_index_in_dim(dealt, core, 0, keepdims=False)
    got = swap_cores(lax.dynamic_index_in_dim(dealt, 1 - core, 0, keepdims=False))
    dealt = joined(core, kept, got)

    def dealt_of(panel):
        return lax.dynamic_index_in_dim(dealt, panel % subset_count, 1, keepdims=False)

    def sensitivity(index, tiles):
        return call(sensitivity_kernel, {"index": index, "tiles": tiles},
                    {"inverse": shaped((both, 8, size), f32)},
                    [pltpu.VMEM((both, 8, size), f32)])["inverse"]

    sets = [(index, tiles, sensitivity(index, tiles))] * ROUNDS
    moves = [True] * (ROUNDS - 1)
    known = [None] * ROUNDS
    two = subset_count == 2
    if two:
        moves = [r == 0 for r in range(ROUNDS - 1)]

    low_scratch, back_scratch = pltpu.VMEM((both, half, size), bf16), pltpu.VMEM((both, half, size), f32)
    ray_scratch, sum_scratch = (pltpu.VMEM((ray_blocks, half, size), kind) for kind in (bf16, f32))
    piece = shaped((half, voxels), f32)
    summed = shaped((ray_blocks, half, size), f32)

    def only(k, pair):
        return tuple(value if i == k else None for i, value in enumerate(pair))

    def sums(r):
        fresh = known[r] is None
        sent = ray_blocks + fresh * rb_dev * CORES
        return ({"dealt": dealt_of(position - r)} if fresh else {},
                {"wide": summed, "sent": shaped((sent, half, size), bf16)})

    extra, outs = sums(0)
    out = call(first_kernel, {"held": held, "index": index, "own_hbm": own_tiles, "tiles": tiles[1], **extra},
               outs, [low_scratch, sum_scratch, pltpu.VMEM(own_tiles.shape, bf16), pltpu.SemaphoreType.DMA])
    for r in range(ROUNDS):
        wide, sent = out["wide"], out["sent"]
        if two and r == 0:
            far_tiles = [shift(after(own_tiles[:slots // 2], sent))]
        if two and r == 1:
            far_index = (far_index, swap_cores(after(far_index, sent)))
            far_swapped = [swap_cores(after(far_tiles[0], sent))]
        for masks in steps:
            got = [swap_chips(sent, mask) for mask in masks]
            if masks is not steps[-1]:
                wide = wide + sum(part[:ray_blocks].astype(f32) for part in got)
                own, counted = place(masks), wide.astype(bf16)
                if sent.shape[0] > ray_blocks:
                    parts = dict(zip((0,) + masks, [sent] + got))
                    ordered = [parts[m * min(masks)][ray_blocks:] for m in range(len(parts))]
                    if len(ordered) == 2:
                        passed = joined(own, *ordered)
                    else:
                        passed = jnp.concatenate([lax.dynamic_index_in_dim(
                            jnp.stack(ordered), own ^ v, 0, keepdims=False) for v in range(len(ordered))])
                    counted = jnp.concatenate([counted, passed])
                sent = counted
        if two and r == 1:
            far_swapped.append(swap_cores(after(far_tiles[1], wide)))
            far_tiles = (tuple(far_tiles), tuple(far_swapped))
            far = (far_index, far_tiles, sensitivity(far_index, far_tiles))
            sets = [far if later >= 2 and later % 2 == 0 else sets[later] for later in range(ROUNDS)]
        now_index, now_tiles, now_inverse = sets[r]
        base = {"index": now_index, "inverse": now_inverse}
        ins = {"wide": wide, "got": got, **base}
        outs = {}
        if known[r] is None:
            ins["sent"] = sent
            if two:
                outs["counts"] = summed.update(dtype=bf16)
        else:
            ins["counts"] = known[r]
        kernel = functools.partial(update_kernel, tuple(m // min(masks) for m in masks))
        last = r + 1 == ROUNDS
        if last or moves[r]:
            order = (1, 0) if last else (0, 1)
            moved, ratios = {}, None
            for k in order:
                if ratios is None:
                    out = call(kernel, {**ins, "held": only(k, held), "tiles": only(k, now_tiles)},
                               {"held": only(k, (piece,) * CORES), "ratios": summed.update(dtype=bf16), **outs},
                               [back_scratch, ray_scratch, ray_scratch])
                    ratios = out["ratios"]
                    if two and r == 0:
                        far_counts = shift(out["counts"])
                else:
                    out = {**out, **call(kernel, {**base, "ratios": ratios, "held": only(k, held),
                                                  "tiles": only(k, now_tiles)},
                                         {"held": only(k, (piece,) * CORES)}, [back_scratch])}
                moved[k] = out["held"][k]
                if two and r == 0 and k == 1:
                    far_index = shift(after(own_index, moved[k]))
                    far_tiles.append(shift(after(own_tiles[slots // 2:], moved[k])))
                if not last:
                    moved[k] = shift(moved[k])
                elif k == 1:
                    moved[k] = swap_cores(moved[k])
            if two and r == 0:
                moved[1], far_index, far_tiles[0] = lax.optimization_barrier((moved[1], far_index, far_tiles[0]))
            held = (moved[0], moved[1])
            if not last:
                extra, more = sums(r + 1)
                begun = call(project_kernel, {"held": only(0, held), "index": sets[r + 1][0],
                                              "tiles": only(0, sets[r + 1][1])},
                             {"wide": summed}, [low_scratch, sum_scratch])["wide"]
                out = call(project_kernel, {"held": only(1, held), "index": sets[r + 1][0], "begun": begun,
                                            "tiles": only(1, sets[r + 1][1]), **extra},
                           more, [low_scratch, sum_scratch])
        else:
            if two and r == 1:
                known[r + 1] = far_counts
            extra, more = sums(r + 1)
            ins.update(held=held, tiles=now_tiles, next_index=sets[r + 1][0], next_tiles=sets[r + 1][1], **extra)
            outs.update(held=(piece,) * CORES, **more)
            out = call(kernel, ins, outs, [back_scratch, ray_scratch, ray_scratch, low_scratch, sum_scratch])
            held = out["held"]
            if two and r == 1:
                known = [known[later] if later < 2 else far_counts if later % 2 == 0 else out["counts"]
                         for later in range(ROUNDS)]
    return joined(core, held[0], held[1])


def solution(mesh):
    in_specs = (
        P("subset", "tile"),
        P("subset", "tile", None, None),
        P("subset", "tile"),
        P("subset", "tile"),
        P("subset", "tile"),
        P("subset", None, "tile"),
    )
    return jax.shard_map(shards, mesh=mesh, in_specs=in_specs, out_specs=P("subset", "tile"),
                         check_vma=False)
```

```python
import functools

import jax
import jax.numpy as jnp
from jax import lax
from jax.experimental import pallas as pl
from jax.experimental.pallas import tpu as pltpu
from jax.sharding import PartitionSpec as P

TILE_GROUP = 32
ROUNDS = 4
CORES = 2
LANES = 128
VMEM_LIMIT = 40 * 1024 * 1024


VOX, RAY, LIVE = range(3)


def entry(index, row, t):
    return index[row][0, t] if isinstance(index, tuple) else index[row, t]


def core_here():
    return lax.rem(lax.axis_index("tile"), CORES)


def each_live(index, slots, body):
    live = entry(index, LIVE, 0)
    for group in range(-(-slots // TILE_GROUP)):
        first, last = group * TILE_GROUP, min(slots, (group + 1) * TILE_GROUP)

        @pl.when(group < live)
        def _():
            for t in range(first, last, 2):
                body(tuple(range(t, min(t + 2, last))))


def add_products(acc, left_of, targets, wide, transposed):
    left = jnp.concatenate(left_of, axis=0)
    dims = (((1,), (1,)), ((), ())) if transposed else (((1,), (0,)), ((), ()))
    part = lax.dot_general(left, wide, dims, preferred_element_type=jnp.float32)
    rows, size = acc.shape[1:]
    for i, at in enumerate(targets):
        used = part[i * left_of[i].shape[0]:, i * size:(i + 1) * size][:rows]
        acc[at] = acc[at] + used


def tile_at(tile_refs, t):
    for ref in tile_refs:
        if t < ref.shape[0]:
            return ref[t]
        t -= ref.shape[0]


def slots_of(tile_refs):
    return sum(ref.shape[0] for ref in tile_refs) // TILE_GROUP * TILE_GROUP


def project_into(acc, low, index_refs, sets):
    blocks = low.shape[0] // CORES
    for k in range(CORES):
        if sets[k] is None:
            continue
        index_ref, tile_refs = index_refs[k], sets[k]

        def body(ts):
            wide = jnp.concatenate([tile_at(tile_refs, t) for t in ts], axis=0)
            add_products(acc, [low[k * blocks + entry(index_ref, VOX, t)] for t in ts],
                         [entry(index_ref, RAY, t) for t in ts], wide, True)

        each_live(index_ref, slots_of(tile_refs), body)


def back_into(acc, ratios, index_refs, sets):
    blocks = acc.shape[0] // CORES
    acc[...] = jnp.zeros_like(acc)
    for k in range(CORES):
        if sets[k] is None:
            continue
        index_ref, tile_refs = index_refs[k], sets[k]

        def body(ts):
            wide = jnp.concatenate([tile_at(tile_refs, t) for t in ts], axis=1)
            add_products(acc, [ratios(entry(index_ref, RAY, t)) for t in ts],
                         [k * blocks + entry(index_ref, VOX, t) for t in ts], wide, False)

        each_live(index_ref, slots_of(tile_refs), body)


def columns(held, size):
    for k in range(CORES):
        if held[k] is not None:
            blocks = held[k].shape[1] // size
            for b in range(blocks):
                yield k, slice(b * size, (b + 1) * size), k * blocks + b


def frames_of(held, half, cols):
    if held.shape[0] == half:
        return held[:, cols]
    return held[pl.ds(pl.multiple_of(core_here() * half, half), half), cols]


def write_sums(r, ins, outs, acc):
    rays, half, size = acc.shape
    outs["wide"][...] = acc[...]
    if "sent" in outs:
        outs["sent"][:rays] = acc[...].astype(jnp.bfloat16)
    if "dealt" in ins:
        core, frames = core_here(), CORES * half
        subsets = ins["dealt"][0].shape[0] // frames
        panel = lax.rem(lax.axis_index("subset") - r + subsets * ROUNDS, subsets)
        rows = pl.ds(pl.multiple_of(panel * frames + core * half, half), half)
        for side, ref in zip((core, 1 - core), ins["dealt"]):
            held = ref.shape[1] // size
            for b in range(held):
                block = ref[rows, b * size:(b + 1) * size].astype(jnp.float32)
                outs["sent"][rays + side * held + b] = block.astype(jnp.bfloat16)


def first_kernel(ins, outs, low, acc, own, arrived):
    copy = pltpu.make_async_copy(ins["own_hbm"], own, arrived)
    copy.start()
    for k, cols, at in columns(ins["held"], low.shape[-1]):
        low[at] = frames_of(ins["held"][k], low.shape[1], cols).astype(jnp.bfloat16)
    acc[...] = jnp.zeros_like(acc)
    project_into(acc, low, ins["index"], (None, ins["tiles"]))
    copy.wait()
    project_into(acc, low, ins["index"], ((own,), None))
    write_sums(0, ins, outs, acc)


def project_kernel(r, ins, outs, low, acc):
    acc[...] = ins["begun"][...] if "begun" in ins else jnp.zeros_like(acc)
    for k, cols, at in columns(ins["held"], low.shape[-1]):
        low[at] = ins["held"][k][:, cols].astype(jnp.bfloat16)
    project_into(acc, low, ins["index"], ins["tiles"])
    write_sums(r, ins, outs, acc)


def sensitivity_kernel(ins, outs, acc):
    ones = jnp.ones((16, ins["tiles"][0][0].shape[1]), jnp.bfloat16)
    back_into(acc, lambda ray: ones, ins["index"], ins["tiles"])
    outs["inverse"][...] = 1.0 / acc[...]


def form_ratios(masks, ins, outs, counts, ratios):
    rays = ratios.shape[0]
    total = ins["wide"][...]
    for got in ins["got"]:
        total = total + got[:rays].astype(jnp.float32)
    if "counts" in ins:
        counts[...] = ins["counts"][...]
    else:
        unit = min(masks)
        place = lax.rem(lax.div(lax.axis_index("tile"), CORES * unit), len(masks) + 1)
        share = ins["sent"].shape[0] - rays
        for mask, part in zip((0,) + masks, (ins["sent"],) + tuple(ins["got"])):
            counts[pl.ds((place ^ mask // unit) * share, share)] = part[rays:]
    if "counts" in outs:
        outs["counts"][...] = counts[...]
    ratios[...] = (counts[...].astype(jnp.float32) / total).astype(jnp.bfloat16)
    if "ratios" in outs:
        outs["ratios"][...] = ratios[...]


def update_kernel(masks, r, ins, outs, back, *scratch):
    if "ratios" in ins:
        ratios = ins["ratios"]
    else:
        counts, ratios, *scratch = scratch
        form_ratios(masks, ins, outs, counts, ratios)
    back_into(back, lambda ray: ratios[ray], ins["index"], ins["tiles"])
    for k, cols, at in columns(ins["held"], back.shape[-1]):
        value = frames_of(ins["held"][k], back.shape[1], cols) * back[at] * ins["inverse"][at, :1]
        outs["held"][k][:, cols] = value
        if "sent" in outs:
            scratch[0][at] = value.astype(jnp.bfloat16)
    if "sent" in outs:
        scratch[1][...] = jnp.zeros_like(scratch[1])
        project_into(scratch[1], scratch[0], ins["next_index"], ins["next_tiles"])
        write_sums(r + 1, ins, outs, scratch[1])


def call(kernel, ins, outs, scratch):
    work = 2 * 256 * 256 * 128 * 32

    def spec(path, _):
        name = path[0].key
        space = pltpu.SMEM if name.endswith("index") else pltpu.HBM if name.endswith("hbm") else pltpu.VMEM
        return pl.BlockSpec(memory_space=space)

    return pl.pallas_call(
        kernel,
        out_shape=outs,
        in_specs=[jax.tree_util.tree_map_with_path(spec, ins)],
        out_specs=jax.tree_util.tree_map_with_path(spec, outs),
        scratch_shapes=scratch,
        cost_estimate=pl.CostEstimate(flops=work * len(jax.tree.leaves(ins.get("tiles"))), transcendentals=0,
                                      bytes_accessed=0),
        compiler_params=pltpu.CompilerParams(vmem_limit_bytes=VMEM_LIMIT))(ins)


def shards(images, system_tiles, tile_vox, tile_ray, live_blocks, counts):
    frames, voxels = images.shape
    half = frames // CORES
    size = system_tiles.shape[-1]
    vox_blocks = voxels // size
    own_tiles = system_tiles[0]
    slots = own_tiles.shape[0]
    assert slots % TILE_GROUP == 0
    tile_devs = lax.axis_size("tile")
    chips = tile_devs // CORES
    rb_dev = counts.shape[2] // size
    ray_blocks = rb_dev * tile_devs
    subset_count = lax.axis_size("subset")
    core = lax.axis_index("tile") % CORES
    chip = lax.axis_index("tile") // CORES
    both = CORES * vox_blocks
    f32, bf16 = jnp.float32, jnp.bfloat16
    shaped = jax.ShapeDtypeStruct

    steps, bit = [], 1
    while bit < chips:
        wide_step = bit * 4 <= chips
        steps.append((bit, 2 * bit, 3 * bit) if wide_step else (bit,))
        bit *= 4 if wide_step else 2

    def place(masks):
        return chip // min(masks) % (len(masks) + 1)

    def swap_cores(array):
        return lax.ppermute(array, "tile", [(i, i ^ 1) for i in range(tile_devs)])

    def swap_chips(array, mask):
        pairs = [(CORES * j + c, CORES * (j ^ mask) + c) for j in range(chips) for c in range(CORES)]
        return lax.ppermute(array, "tile", pairs)

    def joined(side, own, other):
        return jnp.where(side == 0, jnp.concatenate([own, other]), jnp.concatenate([other, own]))

    def shift(array):
        return lax.ppermute(array, "subset", [(i, (i + 1) % subset_count) for i in range(subset_count)])

    def after(array, value):
        return lax.optimization_barrier((array, value))[0]

    rows = (tile_vox, tile_ray, live_blocks)
    tiles = ((own_tiles,), (swap_cores(own_tiles),))
    held = (images, swap_cores(images))
    index = (rows, tuple(swap_cores(row) for row in rows))
    dealt = (counts[0], swap_cores(counts[0]))

    def sensitivity(index, tiles):
        return call(sensitivity_kernel, {"index": index, "tiles": tiles},
                    {"inverse": shaped((both, 8, size), f32)},
                    [pltpu.VMEM((both, 8, size), f32)])["inverse"]

    sets = [(index, tiles, sensitivity(index, tiles))] * ROUNDS
    moves = [True] * (ROUNDS - 1)
    known = [None] * ROUNDS
    two = subset_count == 2 and ray_blocks <= 256 and slots <= size and size == LANES
    early = slots * 11 // 16
    def packed(rows):
        rows = jnp.concatenate([jnp.broadcast_to(row, (1, slots)) for row in rows], axis=0)
        return jnp.pad(rows.astype(bf16), ((0, size - 3), (0, size - slots)))[None]

    def index_of(pieces):
        return pieces[-1][-1, :8].astype(jnp.int32)

    if two:
        far_tiles = [shift(own_tiles[:early])]
    if two:
        moves = [r == 0 for r in range(ROUNDS - 1)]

    low_scratch, back_scratch = pltpu.VMEM((both, half, size), bf16), pltpu.VMEM((both, half, size), f32)
    ray_scratch, sum_scratch = (pltpu.VMEM((ray_blocks, half, size), kind) for kind in (bf16, f32))
    piece = shaped((half, voxels), f32)
    summed = shaped((ray_blocks, half, size), f32)

    def only(k, pair):
        return tuple(value if i == k else None for i, value in enumerate(pair))

    def sums(r):
        fresh = known[r] is None
        sent = ray_blocks + fresh * rb_dev * CORES
        return ({"dealt": dealt} if fresh else {},
                {"wide": summed, "sent": shaped((sent, half, size), bf16)})

    extra, outs = sums(0)
    out = call(first_kernel, {"held": held, "index": index, "own_hbm": own_tiles, "tiles": tiles[1], **extra},
               outs, [low_scratch, sum_scratch, pltpu.VMEM(own_tiles.shape, bf16), pltpu.SemaphoreType.DMA])
    for r in range(ROUNDS):
        wide, sent = out["wide"], out["sent"]
        if two and r == 1:
            far_swapped = [swap_cores(after(far_tiles[0], sent))]
        for masks in steps:
            got = [swap_chips(sent, mask) for mask in masks]
            if masks is not steps[-1]:
                wide = wide + sum(part[:ray_blocks].astype(f32) for part in got)
                own, counted = place(masks), wide.astype(bf16)
                if sent.shape[0] > ray_blocks:
                    parts = dict(zip((0,) + masks, [sent] + got))
                    ordered = [parts[m * min(masks)][ray_blocks:] for m in range(len(parts))]
                    if len(ordered) == 2:
                        passed = joined(own, *ordered)
                    else:
                        passed = jnp.concatenate([lax.dynamic_index_in_dim(
                            jnp.stack(ordered), own ^ v, 0, keepdims=False) for v in range(len(ordered))])
                    counted = jnp.concatenate([counted, passed])
                sent = counted
        if two and r == 1:
            far_swapped.append(swap_cores(after(far_tiles[1], wide)))
            far_tiles = (tuple(far_tiles), tuple(far_swapped))
            far_index = tuple(index_of(pieces) for pieces in far_tiles)
            far = (far_index, far_tiles, sensitivity(far_index, far_tiles))
            sets = [far if later >= 2 and later % 2 == 0 else sets[later] for later in range(ROUNDS)]
        now_index, now_tiles, now_inverse = sets[r]
        base = {"index": now_index, "inverse": now_inverse}
        ins = {"wide": wide, "got": got, **base}
        outs = {}
        if known[r] is None:
            ins["sent"] = sent
            if two:
                outs["counts"] = summed.update(dtype=bf16)
        else:
            ins["counts"] = known[r]
        kernel = functools.partial(update_kernel, masks, r)
        last = r + 1 == ROUNDS
        if last or moves[r]:
            order = (1, 0) if last else (0, 1)
            moved, ratios = {}, None
            for k in order:
                if ratios is None:
                    out = call(kernel, {**ins, "held": only(k, held), "tiles": only(k, now_tiles)},
                               {"held": only(k, (piece,) * CORES), "ratios": summed.update(dtype=bf16), **outs},
                               [back_scratch, ray_scratch, ray_scratch])
                    ratios = out["ratios"]
                    if two and r == 0:
                        far_counts = shift(out["counts"])
                else:
                    out = {**out, **call(kernel, {**base, "ratios": ratios, "held": only(k, held),
                                                  "tiles": only(k, now_tiles)},
                                         {"held": only(k, (piece,) * CORES)}, [back_scratch])}
                moved[k] = out["held"][k]
                if two and r == 0 and k == 1:
                    far_tiles.append(shift(after(jnp.concatenate([own_tiles[early:], packed(after(rows, sent))]), moved[k])))
                if not last:
                    moved[k] = shift(moved[k])
                elif k == 1:
                    moved[k] = swap_cores(moved[k])
            held = (moved[0], moved[1])
            if not last:
                extra, more = sums(r + 1)
                begun = call(functools.partial(project_kernel, r + 1), {"held": only(0, held), "index": sets[r + 1][0],
                                              "tiles": only(0, sets[r + 1][1])},
                             {"wide": summed}, [low_scratch, sum_scratch])["wide"]
                out = call(functools.partial(project_kernel, r + 1), {"held": only(1, held), "index": sets[r + 1][0], "begun": begun,
                                            "tiles": only(1, sets[r + 1][1]), **extra},
                           more, [low_scratch, sum_scratch])
        else:
            if two and r == 1:
                known[r + 1] = far_counts
            extra, more = sums(r + 1)
            ins.update(held=held, tiles=now_tiles, next_index=sets[r + 1][0], next_tiles=sets[r + 1][1], **extra)
            outs.update(held=(piece,) * CORES, **more)
            out = call(kernel, ins, outs, [back_scratch, ray_scratch, ray_scratch, low_scratch, sum_scratch])
            held = out["held"]
            if two and r == 1:
                known = [known[later] if later < 2 else far_counts if later % 2 == 0 else out["counts"]
                         for later in range(ROUNDS)]
    return joined(core, held[0], held[1])


def solution(mesh):
    in_specs = (
        P("subset", "tile"),
        P("subset", "tile", None, None),
        P("subset", "tile"),
        P("subset", "tile"),
        P("subset", "tile"),
        P("subset", None, "tile"),
    )
    return jax.shard_map(shards, mesh=mesh, in_specs=in_specs, out_specs=P("subset", "tile"),
                         check_vma=False)
```

```python
import functools

import jax
import jax.numpy as jnp
from jax import lax
from jax.experimental import pallas as pl
from jax.experimental.pallas import tpu as pltpu
from jax.sharding import PartitionSpec as P

TILE_GROUP = 32
ROUNDS = 4
CORES = 2
LANES = 128
VMEM_LIMIT = 40 * 1024 * 1024


VOX, RAY, LIVE = range(3)


def entry(index, k, row, t):
    return index[k][row, t] if isinstance(index, tuple) else index[3 * k + row, t]


def core_here():
    return lax.rem(lax.axis_index("tile"), CORES)


def each_live(index, k, slots, body):
    live = entry(index, k, LIVE, 0)
    for group in range(-(-slots // TILE_GROUP)):
        first, last = group * TILE_GROUP, min(slots, (group + 1) * TILE_GROUP)

        @pl.when(group < live)
        def _():
            for t in range(first, last, 2):
                body(tuple(range(t, min(t + 2, last))))


def add_products(acc, left_of, targets, wide, transposed):
    left = jnp.concatenate(left_of, axis=0)
    dims = (((1,), (1,)), ((), ())) if transposed else (((1,), (0,)), ((), ()))
    part = lax.dot_general(left, wide, dims, preferred_element_type=jnp.float32)
    rows, size = acc.shape[1:]
    for i, at in enumerate(targets):
        used = part[i * left_of[i].shape[0]:, i * size:(i + 1) * size][:rows]
        acc[at] = acc[at] + used


def tile_at(tile_refs, t):
    for ref in tile_refs:
        if t < ref.shape[0]:
            return ref[t]
        t -= ref.shape[0]


def slots_of(tile_refs):
    return sum(ref.shape[0] for ref in tile_refs) // TILE_GROUP * TILE_GROUP


def project_into(acc, low, index, sets):
    blocks = low.shape[0] // CORES
    for k in range(CORES):
        if sets[k] is None:
            continue
        tile_refs = sets[k]

        def body(ts, k=k, tile_refs=tile_refs):
            wide = jnp.concatenate([tile_at(tile_refs, t) for t in ts], axis=0)
            add_products(acc, [low[k * blocks + entry(index, k, VOX, t)] for t in ts],
                         [entry(index, k, RAY, t) for t in ts], wide, True)

        each_live(index, k, slots_of(tile_refs), body)


def back_into(acc, ratios, index, sets):
    blocks = acc.shape[0] // CORES
    acc[...] = jnp.zeros_like(acc)
    for k in range(CORES):
        if sets[k] is None:
            continue
        tile_refs = sets[k]

        def body(ts, k=k, tile_refs=tile_refs):
            wide = jnp.concatenate([tile_at(tile_refs, t) for t in ts], axis=1)
            add_products(acc, [ratios(entry(index, k, RAY, t)) for t in ts],
                         [k * blocks + entry(index, k, VOX, t) for t in ts], wide, False)

        each_live(index, k, slots_of(tile_refs), body)


def columns(held, size):
    for k in range(CORES):
        if held[k] is not None:
            blocks = held[k].shape[1] // size
            for b in range(blocks):
                yield k, slice(b * size, (b + 1) * size), k * blocks + b


def frames_of(held, half, cols):
    if held.shape[0] == half:
        return held[:, cols]
    return held[pl.ds(pl.multiple_of(core_here() * half, half), half), cols]


def write_sums(r, ins, outs, acc):
    rays, half, size = acc.shape
    outs["wide"][...] = acc[...]
    if "sent" in outs:
        outs["sent"][:rays] = acc[...].astype(jnp.bfloat16)
    if "dealt" in ins:
        core, frames = core_here(), CORES * half
        subsets = ins["dealt"][0].shape[0] // frames
        panel = lax.rem(lax.axis_index("subset") - r + subsets * ROUNDS, subsets)
        rows = pl.ds(pl.multiple_of(panel * frames + core * half, half), half)
        for side, ref in zip((core, 1 - core), ins["dealt"]):
            held = ref.shape[1] // size
            for b in range(held):
                block = ref[rows, b * size:(b + 1) * size].astype(jnp.float32)
                outs["sent"][rays + side * held + b] = block.astype(jnp.bfloat16)


def first_kernel(ins, outs, low, acc, own, arrived):
    copy = pltpu.make_async_copy(ins["own_hbm"], own, arrived)
    copy.start()
    for k, cols, at in columns(ins["held"], low.shape[-1]):
        low[at] = frames_of(ins["held"][k], low.shape[1], cols).astype(jnp.bfloat16)
    acc[...] = jnp.zeros_like(acc)
    project_into(acc, low, ins["index"], (None, ins["tiles"]))
    copy.wait()
    project_into(acc, low, ins["index"], ((own,), None))
    write_sums(0, ins, outs, acc)


def project_kernel(r, ins, outs, low, acc):
    acc[...] = ins["begun"][...] if "begun" in ins else jnp.zeros_like(acc)
    for k, cols, at in columns(ins["held"], low.shape[-1]):
        low[at] = ins["held"][k][:, cols].astype(jnp.bfloat16)
    project_into(acc, low, ins["index"], ins["tiles"])
    write_sums(r, ins, outs, acc)


def sensitivity_kernel(ins, outs, acc):
    ones = jnp.ones((16, ins["tiles"][0][0].shape[1]), jnp.bfloat16)
    back_into(acc, lambda ray: ones, ins["index"], ins["tiles"])
    outs["inverse"][...] = 1.0 / acc[...]


def form_ratios(masks, ins, outs, counts, ratios):
    rays = ratios.shape[0]
    total = ins["wide"][...]
    for got in ins["got"]:
        total = total + got[:rays].astype(jnp.float32)
    if "counts" in ins:
        counts[...] = ins["counts"][...]
    else:
        unit = min(masks)
        place = lax.rem(lax.div(lax.axis_index("tile"), CORES * unit), len(masks) + 1)
        share = ins["sent"].shape[0] - rays
        for mask, part in zip((0,) + masks, (ins["sent"],) + tuple(ins["got"])):
            counts[pl.ds((place ^ mask // unit) * share, share)] = part[rays:]
    if "counts" in outs:
        outs["counts"][...] = counts[...]
    ratios[...] = (counts[...].astype(jnp.float32) / total).astype(jnp.bfloat16)
    if "ratios" in outs:
        outs["ratios"][...] = ratios[...]


def update_kernel(masks, r, ins, outs, back, *scratch):
    if "ratios" in ins:
        ratios = ins["ratios"]
    else:
        counts, ratios, *scratch = scratch
        form_ratios(masks, ins, outs, counts, ratios)
    back_into(back, lambda ray: ratios[ray], ins["index"], ins["tiles"])
    for k, cols, at in columns(ins["held"], back.shape[-1]):
        value = frames_of(ins["held"][k], back.shape[1], cols) * back[at] * ins["inverse"][at, :1]
        outs["held"][k][:, cols] = value
        if "sent" in outs:
            scratch[0][at] = value.astype(jnp.bfloat16)
    if "sent" in outs:
        scratch[1][...] = jnp.zeros_like(scratch[1])
        project_into(scratch[1], scratch[0], ins["next_index"], ins["next_tiles"])
        write_sums(r + 1, ins, outs, scratch[1])


def call(kernel, ins, outs, scratch):
    work = 2 * 256 * 256 * 128 * 32

    def spec(path, _):
        name = path[0].key
        space = pltpu.SMEM if name.endswith("index") else pltpu.HBM if name.endswith("hbm") else pltpu.VMEM
        return pl.BlockSpec(memory_space=space)

    return pl.pallas_call(
        kernel,
        out_shape=outs,
        in_specs=[jax.tree_util.tree_map_with_path(spec, ins)],
        out_specs=jax.tree_util.tree_map_with_path(spec, outs),
        scratch_shapes=scratch,
        cost_estimate=pl.CostEstimate(flops=work * len(jax.tree.leaves(ins.get("tiles"))), transcendentals=0,
                                      bytes_accessed=0),
        compiler_params=pltpu.CompilerParams(vmem_limit_bytes=VMEM_LIMIT))(ins)


def shards(images, system_tiles, tile_vox, tile_ray, live_blocks, counts):
    frames, voxels = images.shape
    half = frames // CORES
    size = system_tiles.shape[-1]
    vox_blocks = voxels // size
    own_tiles = system_tiles[0]
    slots = own_tiles.shape[0]
    assert slots % TILE_GROUP == 0
    tile_devs = lax.axis_size("tile")
    chips = tile_devs // CORES
    rb_dev = counts.shape[2] // size
    ray_blocks = rb_dev * tile_devs
    subset_count = lax.axis_size("subset")
    core = lax.axis_index("tile") % CORES
    chip = lax.axis_index("tile") // CORES
    both = CORES * vox_blocks
    f32, bf16 = jnp.float32, jnp.bfloat16
    shaped = jax.ShapeDtypeStruct

    steps, bit = [], 1
    while bit < chips:
        wide_step = bit * 4 <= chips
        steps.append((bit, 2 * bit, 3 * bit) if wide_step else (bit,))
        bit *= 4 if wide_step else 2

    def place(masks):
        return chip // min(masks) % (len(masks) + 1)

    def swap_cores(array):
        return lax.ppermute(array, "tile", [(i, i ^ 1) for i in range(tile_devs)])

    def swap_chips(array, mask):
        pairs = [(CORES * j + c, CORES * (j ^ mask) + c) for j in range(chips) for c in range(CORES)]
        return lax.ppermute(array, "tile", pairs)

    def joined(side, own, other):
        return jnp.where(side == 0, jnp.concatenate([own, other]), jnp.concatenate([other, own]))

    def shift(array):
        return lax.ppermute(array, "subset", [(i, (i + 1) % subset_count) for i in range(subset_count)])

    def after(array, value):
        return lax.optimization_barrier((array, value))[0]

    rows = jnp.concatenate([tile_vox, tile_ray, jnp.broadcast_to(live_blocks, tile_vox.shape)], axis=0)
    own_index = jnp.pad(rows, ((0, 5), (0, -slots % LANES)))
    tiles = ((own_tiles,), (swap_cores(own_tiles),))
    held = (images, swap_cores(images))
    first_index = (own_index, swap_cores(own_index))

    def merged(own, other):
        return jnp.concatenate([own[:3], other[:3], jnp.zeros_like(own[:2])])

    index = merged(*first_index)
    dealt = (counts[0], swap_cores(counts[0]))

    def sensitivity(index, tiles):
        return call(sensitivity_kernel, {"index": index, "tiles": tiles},
                    {"inverse": shaped((both, 8, size), f32)},
                    [pltpu.VMEM((both, 8, size), f32)])["inverse"]

    sets = [(index, tiles, sensitivity(index, tiles))] * ROUNDS
    moves = [True] * (ROUNDS - 1)
    known = [None] * ROUNDS
    two = subset_count == 2 and ray_blocks <= 256 and slots <= size and size == LANES
    late = slots // 2
    if two:
        moves = [r == 0 for r in range(ROUNDS - 1)]

    low_scratch, back_scratch = pltpu.VMEM((both, half, size), bf16), pltpu.VMEM((both, half, size), f32)
    ray_scratch, sum_scratch = (pltpu.VMEM((ray_blocks, half, size), kind) for kind in (bf16, f32))
    piece = shaped((half, voxels), f32)
    summed = shaped((ray_blocks, half, size), f32)

    def only(k, pair):
        return tuple(value if i == k else None for i, value in enumerate(pair))

    def sums(r):
        fresh = known[r] is None
        sent = ray_blocks + fresh * rb_dev * CORES
        return ({"dealt": dealt} if fresh else {},
                {"wide": summed, "sent": shaped((sent, half, size), bf16)})

    extra, outs = sums(0)
    out = call(first_kernel, {"held": held, "index": first_index, "own_hbm": own_tiles, "tiles": tiles[1], **extra},
               outs, [low_scratch, sum_scratch, pltpu.VMEM(own_tiles.shape, bf16), pltpu.SemaphoreType.DMA])
    for r in range(ROUNDS):
        wide, sent = out["wide"], out["sent"]
        if two and r == 0:
            tiles_then, rows_then = after((own_tiles[late:], own_index), sent)
            slot = jnp.pad(rows_then.astype(bf16), ((0, size - 8), (0, 0)))[None]
            far_second = shift(jnp.concatenate([tiles_then, slot]))
        if two and r == 1:
            other_second = swap_cores(after(far_second, sent))
        for masks in steps:
            got = [swap_chips(sent, mask) for mask in masks]
            if masks is not steps[-1]:
                wide = wide + sum(part[:ray_blocks].astype(f32) for part in got)
                own, counted = place(masks), wide.astype(bf16)
                if sent.shape[0] > ray_blocks:
                    parts = dict(zip((0,) + masks, [sent] + got))
                    ordered = [parts[m * min(masks)][ray_blocks:] for m in range(len(parts))]
                    if len(ordered) == 2:
                        passed = joined(own, *ordered)
                    else:
                        passed = jnp.concatenate([lax.dynamic_index_in_dim(
                            jnp.stack(ordered), own ^ v, 0, keepdims=False) for v in range(len(ordered))])
                    counted = jnp.concatenate([counted, passed])
                sent = counted
        if two and r == 1:
            other_first = swap_cores(after(far_first, tuple(got)))
            far_tiles = ((far_first, far_second), (other_first, other_second))
            far_index = merged(*(piece[-1, :8].astype(jnp.int32) for piece in (far_second, other_second)))
            far = (far_index, far_tiles, sensitivity(far_index, far_tiles))
            sets = [far if later >= 2 and later % 2 == 0 else sets[later] for later in range(ROUNDS)]
        now_index, now_tiles, now_inverse = sets[r]
        base = {"index": now_index, "inverse": now_inverse}
        ins = {"wide": wide, "got": got, **base}
        outs = {}
        if known[r] is None:
            ins["sent"] = sent
            if two:
                outs["counts"] = summed.update(dtype=bf16)
        else:
            ins["counts"] = known[r]
        kernel = functools.partial(update_kernel, masks, r)
        last = r + 1 == ROUNDS
        if last or moves[r]:
            order = (1, 0) if last else (0, 1)
            moved, ratios = {}, None
            for k in order:
                if ratios is None:
                    out = call(kernel, {**ins, "held": only(k, held), "tiles": only(k, now_tiles)},
                               {"held": only(k, (piece,) * CORES), "ratios": summed.update(dtype=bf16), **outs},
                               [back_scratch, ray_scratch, ray_scratch])
                    ratios = out["ratios"]
                    if two and r == 0:
                        far_counts = shift(out["counts"])
                else:
                    out = {**out, **call(kernel, {**base, "ratios": ratios, "held": only(k, held),
                                                  "tiles": only(k, now_tiles)},
                                         {"held": only(k, (piece,) * CORES)}, [back_scratch])}
                moved[k] = out["held"][k]
                if two and r == 0 and k == 1:
                    far_first = shift(after(own_tiles[:late], moved[k]))
                if not last:
                    moved[k] = shift(moved[k])
                elif k == 1:
                    moved[k] = swap_cores(moved[k])
            if two and r == 0:
                moved[1], far_second = lax.optimization_barrier((moved[1], far_second))
            held = (moved[0], moved[1])
            if not last:
                extra, more = sums(r + 1)
                begun = call(functools.partial(project_kernel, r + 1), {"held": only(0, held), "index": sets[r + 1][0],
                                              "tiles": only(0, sets[r + 1][1])},
                             {"wide": summed}, [low_scratch, sum_scratch])["wide"]
                out = call(functools.partial(project_kernel, r + 1), {"held": only(1, held), "index": sets[r + 1][0], "begun": begun,
                                            "tiles": only(1, sets[r + 1][1]), **extra},
                           more, [low_scratch, sum_scratch])
        else:
            if two and r == 1:
                known[r + 1] = far_counts
            extra, more = sums(r + 1)
            ins.update(held=held, tiles=now_tiles)
            outs.update(held=(piece,) * CORES)
            if two and r == 1:
                out = call(kernel, ins, outs, [back_scratch, ray_scratch, ray_scratch])
                then = call(functools.partial(project_kernel, r + 1),
                            {"held": out["held"], "index": sets[r + 1][0], "tiles": sets[r + 1][1], **extra},
                            more, [low_scratch, sum_scratch])
                out = {**out, **then}
            else:
                ins.update(next_index=sets[r + 1][0], next_tiles=sets[r + 1][1], **extra)
                outs.update(more)
                out = call(kernel, ins, outs, [back_scratch, ray_scratch, ray_scratch, low_scratch, sum_scratch])
            held = out["held"]
            if two and r == 1:
                known = [known[later] if later < 2 else far_counts if later % 2 == 0 else out["counts"]
                         for later in range(ROUNDS)]
    return joined(core, held[0], held[1])


def solution(mesh):
    in_specs = (
        P("subset", "tile"),
        P("subset", "tile", None, None),
        P("subset", "tile"),
        P("subset", "tile"),
        P("subset", "tile"),
        P("subset", None, "tile"),
    )
    return jax.shard_map(shards, mesh=mesh, in_specs=in_specs, out_specs=P("subset", "tile"),
                         check_vma=False)
```

```python
import functools

import jax
import jax.numpy as jnp
from jax import lax
from jax.experimental import pallas as pl
from jax.experimental.pallas import tpu as pltpu
from jax.sharding import PartitionSpec as P

TILE_GROUP = 32
ROUNDS = 4
CORES = 2
LANES = 128
VMEM_LIMIT = 40 * 1024 * 1024


VOX, RAY, LIVE = range(3)


def entry(index, k, row, t):
    return index[k][row][0, t] if isinstance(index, tuple) else index[3 * k + row, t]


def core_here():
    return lax.rem(lax.axis_index("tile"), CORES)


def each_live(index, k, slots, body):
    live = entry(index, k, LIVE, 0)
    for group in range(-(-slots // TILE_GROUP)):
        first, last = group * TILE_GROUP, min(slots, (group + 1) * TILE_GROUP)

        @pl.when(group < live)
        def _():
            for t in range(first, last, 2):
                body(tuple(range(t, min(t + 2, last))))


def add_products(acc, left_of, targets, wide, transposed):
    left = jnp.concatenate(left_of, axis=0)
    dims = (((1,), (1,)), ((), ())) if transposed else (((1,), (0,)), ((), ()))
    part = lax.dot_general(left, wide, dims, preferred_element_type=jnp.float32)
    rows, size = acc.shape[1:]
    for i, at in enumerate(targets):
        used = part[i * left_of[i].shape[0]:, i * size:(i + 1) * size][:rows]
        acc[at] = acc[at] + used


def tile_at(tile_refs, t):
    for ref in tile_refs:
        if t < ref.shape[0]:
            return ref[t]
        t -= ref.shape[0]


def slots_of(tile_refs):
    return sum(ref.shape[0] for ref in tile_refs) // TILE_GROUP * TILE_GROUP


def project_into(acc, low, index, sets):
    blocks = low.shape[0] // CORES
    for k in range(CORES):
        if sets[k] is None:
            continue
        tile_refs = sets[k]

        def body(ts, k=k, tile_refs=tile_refs):
            wide = jnp.concatenate([tile_at(tile_refs, t) for t in ts], axis=0)
            add_products(acc, [low[k * blocks + entry(index, k, VOX, t)] for t in ts],
                         [entry(index, k, RAY, t) for t in ts], wide, True)

        each_live(index, k, slots_of(tile_refs), body)


def back_into(acc, ratios, index, sets):
    blocks = acc.shape[0] // CORES
    acc[...] = jnp.zeros_like(acc)
    for k in range(CORES):
        if sets[k] is None:
            continue
        tile_refs = sets[k]

        def body(ts, k=k, tile_refs=tile_refs):
            wide = jnp.concatenate([tile_at(tile_refs, t) for t in ts], axis=1)
            add_products(acc, [ratios(entry(index, k, RAY, t)) for t in ts],
                         [k * blocks + entry(index, k, VOX, t) for t in ts], wide, False)

        each_live(index, k, slots_of(tile_refs), body)


def columns(held, size):
    for k in range(CORES):
        if held[k] is not None:
            blocks = held[k].shape[1] // size
            for b in range(blocks):
                yield k, slice(b * size, (b + 1) * size), k * blocks + b


def frames_of(held, half, cols):
    if held.shape[0] == half:
        return held[:, cols]
    return held[pl.ds(pl.multiple_of(core_here() * half, half), half), cols]


def write_sums(r, ins, outs, acc):
    rays, half, size = acc.shape
    outs["wide"][...] = acc[...]
    if "sent" in outs:
        outs["sent"][:rays] = acc[...].astype(jnp.bfloat16)
    if "dealt" in ins:
        core, frames = core_here(), CORES * half
        subsets = ins["dealt"][0].shape[0] // frames
        panel = lax.rem(lax.axis_index("subset") - r + subsets * ROUNDS, subsets)
        rows = pl.ds(pl.multiple_of(panel * frames + core * half, half), half)
        for side, ref in zip((core, 1 - core), ins["dealt"]):
            held = ref.shape[1] // size
            for b in range(held):
                block = ref[rows, b * size:(b + 1) * size].astype(jnp.float32)
                outs["sent"][rays + side * held + b] = block.astype(jnp.bfloat16)


def project_kernel(r, ins, outs, low, acc):
    acc[...] = ins["begun"][...] if "begun" in ins else jnp.zeros_like(acc)
    for k, cols, at in columns(ins["held"], low.shape[-1]):
        low[at] = frames_of(ins["held"][k], low.shape[1], cols).astype(jnp.bfloat16)
    project_into(acc, low, ins["index"], ins["tiles"])
    write_sums(r, ins, outs, acc)


def sensitivity_kernel(ins, outs, acc):
    ones = jnp.ones((16, ins["tiles"][0][0].shape[1]), jnp.bfloat16)
    back_into(acc, lambda ray: ones, ins["index"], ins["tiles"])
    outs["inverse"][...] = 1.0 / acc[...]


def form_ratios(masks, ins, outs, counts, ratios):
    rays = ratios.shape[0]
    total = ins["wide"][...]
    for got in ins["got"]:
        total = total + got[:rays].astype(jnp.float32)
    if "counts" in ins:
        counts[...] = ins["counts"][...]
    else:
        unit = min(masks)
        place = lax.rem(lax.div(lax.axis_index("tile"), CORES * unit), len(masks) + 1)
        share = ins["sent"].shape[0] - rays
        for mask, part in zip((0,) + masks, (ins["sent"],) + tuple(ins["got"])):
            counts[pl.ds((place ^ mask // unit) * share, share)] = part[rays:]
    if "counts" in outs:
        outs["counts"][...] = counts[...]
    ratios[...] = (counts[...].astype(jnp.float32) / total).astype(jnp.bfloat16)
    if "ratios" in outs:
        outs["ratios"][...] = ratios[...]


def update_kernel(masks, r, ins, outs, back, *scratch):
    if "ratios" in ins:
        ratios = ins["ratios"]
    else:
        counts, ratios, *scratch = scratch
        form_ratios(masks, ins, outs, counts, ratios)
    back_into(back, lambda ray: ratios[ray], ins["index"], ins["tiles"])
    for k, cols, at in columns(ins["held"], back.shape[-1]):
        value = frames_of(ins["held"][k], back.shape[1], cols) * back[at] * ins["inverse"][at, :1]
        outs["held"][k][:, cols] = value
        if "sent" in outs:
            scratch[0][at] = value.astype(jnp.bfloat16)
    if "sent" in outs:
        scratch[1][...] = jnp.zeros_like(scratch[1])
        project_into(scratch[1], scratch[0], ins["next_index"], ins["next_tiles"])
        write_sums(r + 1, ins, outs, scratch[1])


def call(kernel, ins, outs, scratch):
    work = 2 * 256 * 256 * 128 * 32

    def spec(path, _):
        name = path[0].key
        space = pltpu.SMEM if name.endswith("index") else pltpu.VMEM
        return pl.BlockSpec(memory_space=space)

    return pl.pallas_call(
        kernel,
        out_shape=outs,
        in_specs=[jax.tree_util.tree_map_with_path(spec, ins)],
        out_specs=jax.tree_util.tree_map_with_path(spec, outs),
        scratch_shapes=scratch,
        cost_estimate=pl.CostEstimate(flops=work * len(jax.tree.leaves(ins.get("tiles"))), transcendentals=0,
                                      bytes_accessed=0),
        compiler_params=pltpu.CompilerParams(vmem_limit_bytes=VMEM_LIMIT))(ins)


def shards(images, system_tiles, tile_vox, tile_ray, live_blocks, counts):
    frames, voxels = images.shape
    half = frames // CORES
    size = system_tiles.shape[-1]
    vox_blocks = voxels // size
    own_tiles = system_tiles[0]
    slots = own_tiles.shape[0]
    assert slots % TILE_GROUP == 0
    tile_devs = lax.axis_size("tile")
    chips = tile_devs // CORES
    rb_dev = counts.shape[2] // size
    ray_blocks = rb_dev * tile_devs
    subset_count = lax.axis_size("subset")
    core = lax.axis_index("tile") % CORES
    chip = lax.axis_index("tile") // CORES
    both = CORES * vox_blocks
    f32, bf16 = jnp.float32, jnp.bfloat16
    shaped = jax.ShapeDtypeStruct

    steps, bit = [], 1
    while bit < chips:
        wide_step = bit * 4 <= chips
        steps.append((bit, 2 * bit, 3 * bit) if wide_step else (bit,))
        bit *= 4 if wide_step else 2

    def place(masks):
        return chip // min(masks) % (len(masks) + 1)

    def swap_cores(array):
        return lax.ppermute(array, "tile", [(i, i ^ 1) for i in range(tile_devs)])

    def swap_chips(array, mask):
        pairs = [(CORES * j + c, CORES * (j ^ mask) + c) for j in range(chips) for c in range(CORES)]
        return lax.ppermute(array, "tile", pairs)

    def joined(side, own, other):
        return jnp.where(side == 0, jnp.concatenate([own, other]), jnp.concatenate([other, own]))

    def shift(array):
        return lax.ppermute(array, "subset", [(i, (i + 1) % subset_count) for i in range(subset_count)])

    def after(array, value):
        return lax.optimization_barrier((array, value))[0]

    rows = (tile_vox, tile_ray, live_blocks)
    tiles = ((own_tiles,), (swap_cores(own_tiles),))
    held = (images, swap_cores(images))
    first_index = (rows, tuple(swap_cores(row) for row in rows))

    def packed(own, other):
        spread = [jnp.broadcast_to(row, (1, slots)) for row in own + other]
        return jnp.pad(jnp.concatenate(spread), ((0, 2), (0, -slots % LANES)))

    dealt = (counts[0], swap_cores(counts[0]))

    def sensitivity(index, tiles):
        return call(sensitivity_kernel, {"index": index, "tiles": tiles},
                    {"inverse": shaped((both, 8, size), f32)},
                    [pltpu.VMEM((both, 8, size), f32)])["inverse"]

    moves = [True] * (ROUNDS - 1)
    known = [None] * ROUNDS
    two = subset_count == 2 and ray_blocks <= 256 and slots <= size and size == LANES
    late = slots * 19 // 32
    if two:
        moves = [r == 0 for r in range(ROUNDS - 1)]

    low_scratch, back_scratch = pltpu.VMEM((both, half, size), bf16), pltpu.VMEM((both, half, size), f32)
    ray_scratch, sum_scratch = (pltpu.VMEM((ray_blocks, half, size), kind) for kind in (bf16, f32))
    piece = shaped((half, voxels), f32)
    summed = shaped((ray_blocks, half, size), f32)

    def only(k, pair):
        return tuple(value if i == k else None for i, value in enumerate(pair))

    def sums(r):
        fresh = known[r] is None
        sent = ray_blocks + fresh * rb_dev * CORES
        return ({"dealt": dealt} if fresh else {},
                {"wide": summed, "sent": shaped((sent, half, size), bf16)})

    extra, outs = sums(0)
    begun = call(functools.partial(project_kernel, 0),
                 {"held": only(0, held), "index": only(0, first_index), "tiles": only(0, tiles)},
                 {"wide": summed}, [low_scratch, sum_scratch])["wide"]
    out = call(functools.partial(project_kernel, 0),
               {"held": only(1, held), "index": only(1, first_index), "tiles": only(1, tiles), "begun": begun, **extra},
               outs, [low_scratch, sum_scratch])
    index = packed(*after(first_index, out["sent"]))
    sets = [(index, tiles, sensitivity(index, tiles))] * ROUNDS
    for r in range(ROUNDS):
        wide, sent = out["wide"], out["sent"]
        if two and r == 0:
            tiles_then = after(own_tiles[late:], sent)
            slot = jnp.pad(index.astype(bf16), ((0, size - 8), (0, 0)))[None]
            far_second = shift(jnp.concatenate([tiles_then, slot]))
        if two and r == 1:
            other_second = swap_cores(after(far_second, sent))
        for masks in steps:
            got = [swap_chips(sent, mask) for mask in masks]
            if masks is not steps[-1]:
                wide = wide + sum(part[:ray_blocks].astype(f32) for part in got)
                own, counted = place(masks), wide.astype(bf16)
                if sent.shape[0] > ray_blocks:
                    parts = dict(zip((0,) + masks, [sent] + got))
                    ordered = [parts[m * min(masks)][ray_blocks:] for m in range(len(parts))]
                    if len(ordered) == 2:
                        passed = joined(own, *ordered)
                    else:
                        passed = jnp.concatenate([lax.dynamic_index_in_dim(
                            jnp.stack(ordered), own ^ v, 0, keepdims=False) for v in range(len(ordered))])
                    counted = jnp.concatenate([counted, passed])
                sent = counted
        if two and r == 1:
            other_first = swap_cores(after(far_first, tuple(got)))
            far_tiles = ((far_first, far_second), (other_first, other_second))
            far_index = far_second[-1, :8].astype(jnp.int32)
            far = (far_index, far_tiles, sensitivity(far_index, far_tiles))
            sets = [far if later >= 2 and later % 2 == 0 else sets[later] for later in range(ROUNDS)]
        now_index, now_tiles, now_inverse = sets[r]
        base = {"index": now_index, "inverse": now_inverse}
        ins = {"wide": wide, "got": got, **base}
        outs = {}
        if known[r] is None:
            ins["sent"] = sent
            if two:
                outs["counts"] = summed.update(dtype=bf16)
        else:
            ins["counts"] = known[r]
        kernel = functools.partial(update_kernel, masks, r)
        last = r + 1 == ROUNDS
        if last or moves[r]:
            order = (1, 0) if last else (0, 1)
            moved, ratios = {}, None
            for k in order:
                if ratios is None:
                    out = call(kernel, {**ins, "held": only(k, held), "tiles": only(k, now_tiles)},
                               {"held": only(k, (piece,) * CORES), "ratios": summed.update(dtype=bf16), **outs},
                               [back_scratch, ray_scratch, ray_scratch])
                    ratios = out["ratios"]
                    if two and r == 0:
                        far_counts = shift(out["counts"])
                else:
                    out = {**out, **call(kernel, {**base, "ratios": ratios, "held": only(k, held),
                                                  "tiles": only(k, now_tiles)},
                                         {"held": only(k, (piece,) * CORES)}, [back_scratch])}
                moved[k] = out["held"][k]
                if two and r == 0 and k == 1:
                    far_first = shift(after(own_tiles[:late], moved[k]))
                if not last:
                    moved[k] = shift(moved[k])
                elif k == 1:
                    moved[k] = swap_cores(moved[k])
            if two and r == 0:
                moved[1], far_second = lax.optimization_barrier((moved[1], far_second))
            held = (moved[0], moved[1])
            if not last:
                extra, more = sums(r + 1)
                begun = call(functools.partial(project_kernel, r + 1), {"held": only(0, held), "index": sets[r + 1][0],
                                              "tiles": only(0, sets[r + 1][1])},
                             {"wide": summed}, [low_scratch, sum_scratch])["wide"]
                out = call(functools.partial(project_kernel, r + 1), {"held": only(1, held), "index": sets[r + 1][0], "begun": begun,
                                            "tiles": only(1, sets[r + 1][1]), **extra},
                           more, [low_scratch, sum_scratch])
        else:
            if two and r == 1:
                known[r + 1] = far_counts
            extra, more = sums(r + 1)
            ins.update(held=held, tiles=now_tiles)
            outs.update(held=(piece,) * CORES)
            if two and r == 1:
                out = call(kernel, ins, outs, [back_scratch, ray_scratch, ray_scratch])
                then = call(functools.partial(project_kernel, r + 1),
                            {"held": out["held"], "index": sets[r + 1][0], "tiles": sets[r + 1][1], **extra},
                            more, [low_scratch, sum_scratch])
                out = {**out, **then}
            else:
                ins.update(next_index=sets[r + 1][0], next_tiles=sets[r + 1][1], **extra)
                outs.update(more)
                out = call(kernel, ins, outs, [back_scratch, ray_scratch, ray_scratch, low_scratch, sum_scratch])
            held = out["held"]
            if two and r == 1:
                known = [known[later] if later < 2 else far_counts if later % 2 == 0 else out["counts"]
                         for later in range(ROUNDS)]
    return joined(core, held[0], held[1])


def solution(mesh):
    in_specs = (
        P("subset", "tile"),
        P("subset", "tile", None, None),
        P("subset", "tile"),
        P("subset", "tile"),
        P("subset", "tile"),
        P("subset", None, "tile"),
    )
    return jax.shard_map(shards, mesh=mesh, in_specs=in_specs, out_specs=P("subset", "tile"),
                         check_vma=False)
```

```python
import functools

import jax
import jax.numpy as jnp
from jax import lax
from jax.experimental import pallas as pl
from jax.experimental.pallas import tpu as pltpu
from jax.sharding import PartitionSpec as P

TILE_GROUP = 32
ROUNDS = 4
CORES = 2
LANES = 128
VMEM_LIMIT = 40 * 1024 * 1024


VOX, RAY, LIVE = range(3)


def entry(index, k, row, t):
    return index[k][row, t] if isinstance(index, tuple) else index[3 * k + row, t]


def core_here():
    return lax.rem(lax.axis_index("tile"), CORES)


def each_live(index, k, slots, body):
    live = entry(index, k, LIVE, 0)
    for group in range(-(-slots // TILE_GROUP)):
        first, last = group * TILE_GROUP, min(slots, (group + 1) * TILE_GROUP)

        @pl.when(group < live)
        def _():
            for t in range(first, last, 2):
                body(tuple(range(t, min(t + 2, last))))


def add_products(acc, left_of, targets, wide, transposed):
    left = jnp.concatenate(left_of, axis=0)
    dims = (((1,), (1,)), ((), ())) if transposed else (((1,), (0,)), ((), ()))
    part = lax.dot_general(left, wide, dims, preferred_element_type=jnp.float32)
    rows, size = acc.shape[1:]
    for i, at in enumerate(targets):
        used = part[i * left_of[i].shape[0]:, i * size:(i + 1) * size][:rows]
        acc[at] = acc[at] + used


def tile_at(tile_refs, t):
    for ref in tile_refs:
        if t < ref.shape[0]:
            return ref[t]
        t -= ref.shape[0]


def slots_of(tile_refs):
    return sum(ref.shape[0] for ref in tile_refs) // TILE_GROUP * TILE_GROUP


def project_into(acc, low, index, sets):
    blocks = low.shape[0] // CORES
    for k in range(CORES):
        if sets[k] is None:
            continue
        tile_refs = sets[k]

        def body(ts, k=k, tile_refs=tile_refs):
            wide = jnp.concatenate([tile_at(tile_refs, t) for t in ts], axis=0)
            add_products(acc, [low[k * blocks + entry(index, k, VOX, t)] for t in ts],
                         [entry(index, k, RAY, t) for t in ts], wide, True)

        each_live(index, k, slots_of(tile_refs), body)


def back_into(acc, ratios, index, sets):
    blocks = acc.shape[0] // CORES
    acc[...] = jnp.zeros_like(acc)
    for k in range(CORES):
        if sets[k] is None:
            continue
        tile_refs = sets[k]

        def body(ts, k=k, tile_refs=tile_refs):
            wide = jnp.concatenate([tile_at(tile_refs, t) for t in ts], axis=1)
            add_products(acc, [ratios(entry(index, k, RAY, t)) for t in ts],
                         [k * blocks + entry(index, k, VOX, t) for t in ts], wide, False)

        each_live(index, k, slots_of(tile_refs), body)


def columns(held, size):
    for k in range(CORES):
        if held[k] is not None:
            blocks = held[k].shape[1] // size
            for b in range(blocks):
                yield k, slice(b * size, (b + 1) * size), k * blocks + b


def frames_of(held, half, cols):
    if held.shape[0] == half:
        return held[:, cols]
    return held[pl.ds(pl.multiple_of(core_here() * half, half), half), cols]


def write_sums(r, ins, outs, acc):
    rays, half, size = acc.shape
    outs["wide"][...] = acc[...]
    if "sent" in outs:
        outs["sent"][:rays] = acc[...].astype(jnp.bfloat16)
    if "dealt" in ins:
        core, frames = core_here(), CORES * half
        subsets = ins["dealt"][0].shape[0] // frames
        panel = lax.rem(lax.axis_index("subset") - r + subsets * ROUNDS, subsets)
        rows = pl.ds(pl.multiple_of(panel * frames + core * half, half), half)
        for side, ref in zip((core, 1 - core), ins["dealt"]):
            held = ref.shape[1] // size
            for b in range(held):
                block = ref[rows, b * size:(b + 1) * size].astype(jnp.float32)
                outs["sent"][rays + side * held + b] = block.astype(jnp.bfloat16)


def first_kernel(ins, outs, low, acc, own, arrived):
    copy = pltpu.make_async_copy(ins["own_hbm"], own, arrived)
    copy.start()
    for k, cols, at in columns(ins["held"], low.shape[-1]):
        low[at] = frames_of(ins["held"][k], low.shape[1], cols).astype(jnp.bfloat16)
    acc[...] = jnp.zeros_like(acc)
    project_into(acc, low, ins["index"], (None, ins["tiles"]))
    copy.wait()
    project_into(acc, low, ins["index"], ((own,), None))
    write_sums(0, ins, outs, acc)


def project_kernel(r, ins, outs, low, acc):
    acc[...] = ins["begun"][...] if "begun" in ins else jnp.zeros_like(acc)
    for k, cols, at in columns(ins["held"], low.shape[-1]):
        low[at] = ins["held"][k][:, cols].astype(jnp.bfloat16)
    project_into(acc, low, ins["index"], ins["tiles"])
    write_sums(r, ins, outs, acc)


def sensitivity_kernel(ins, outs, acc):
    ones = jnp.ones((16, ins["tiles"][0][0].shape[1]), jnp.bfloat16)
    back_into(acc, lambda ray: ones, ins["index"], ins["tiles"])
    outs["inverse"][...] = 1.0 / acc[...]


def form_ratios(masks, ins, outs, counts, ratios):
    rays = ratios.shape[0]
    total = ins["wide"][...]
    for got in ins["got"]:
        total = total + got[:rays].astype(jnp.float32)
    if "counts" in ins:
        counts[...] = ins["counts"][...]
    else:
        unit = min(masks)
        place = lax.rem(lax.div(lax.axis_index("tile"), CORES * unit), len(masks) + 1)
        share = ins["sent"].shape[0] - rays
        for mask, part in zip((0,) + masks, (ins["sent"],) + tuple(ins["got"])):
            counts[pl.ds((place ^ mask // unit) * share, share)] = part[rays:]
    if "counts" in outs:
        outs["counts"][...] = counts[...]
    ratios[...] = (counts[...].astype(jnp.float32) / total).astype(jnp.bfloat16)
    if "ratios" in outs:
        outs["ratios"][...] = ratios[...]


def update_kernel(masks, r, ins, outs, back, *scratch):
    if "ratios" in ins:
        ratios = ins["ratios"]
    else:
        counts, ratios, *scratch = scratch
        form_ratios(masks, ins, outs, counts, ratios)
    back_into(back, lambda ray: ratios[ray], ins["index"], ins["tiles"])
    for k, cols, at in columns(ins["held"], back.shape[-1]):
        value = frames_of(ins["held"][k], back.shape[1], cols) * back[at] * ins["inverse"][at, :1]
        outs["held"][k][:, cols] = value
        if "sent" in outs:
            scratch[0][at] = value.astype(jnp.bfloat16)
    if "sent" in outs:
        scratch[1][...] = jnp.zeros_like(scratch[1])
        project_into(scratch[1], scratch[0], ins["next_index"], ins["next_tiles"])
        write_sums(r + 1, ins, outs, scratch[1])


def call(kernel, ins, outs, scratch):
    work = 2 * 256 * 256 * 128 * 32

    def spec(path, _):
        name = path[0].key
        space = pltpu.SMEM if name.endswith("index") else pltpu.HBM if name.endswith("hbm") else pltpu.VMEM
        return pl.BlockSpec(memory_space=space)

    return pl.pallas_call(
        kernel,
        out_shape=outs,
        in_specs=[jax.tree_util.tree_map_with_path(spec, ins)],
        out_specs=jax.tree_util.tree_map_with_path(spec, outs),
        scratch_shapes=scratch,
        cost_estimate=pl.CostEstimate(flops=work * len(jax.tree.leaves(ins.get("tiles"))), transcendentals=0,
                                      bytes_accessed=0),
        compiler_params=pltpu.CompilerParams(vmem_limit_bytes=VMEM_LIMIT))(ins)


def shards(images, system_tiles, tile_vox, tile_ray, live_blocks, counts):
    frames, voxels = images.shape
    half = frames // CORES
    size = system_tiles.shape[-1]
    vox_blocks = voxels // size
    own_tiles = system_tiles[0]
    slots = own_tiles.shape[0]
    assert slots % TILE_GROUP == 0
    tile_devs = lax.axis_size("tile")
    chips = tile_devs // CORES
    rb_dev = counts.shape[2] // size
    ray_blocks = rb_dev * tile_devs
    subset_count = lax.axis_size("subset")
    core = lax.axis_index("tile") % CORES
    chip = lax.axis_index("tile") // CORES
    both = CORES * vox_blocks
    f32, bf16 = jnp.float32, jnp.bfloat16
    shaped = jax.ShapeDtypeStruct

    steps, bit = [], 1
    while bit < chips:
        wide_step = bit * 4 <= chips
        steps.append((bit, 2 * bit, 3 * bit) if wide_step else (bit,))
        bit *= 4 if wide_step else 2

    def place(masks):
        return chip // min(masks) % (len(masks) + 1)

    def swap_cores(array):
        return lax.ppermute(array, "tile", [(i, i ^ 1) for i in range(tile_devs)])

    def swap_chips(array, mask):
        pairs = [(CORES * j + c, CORES * (j ^ mask) + c) for j in range(chips) for c in range(CORES)]
        return lax.ppermute(array, "tile", pairs)

    def joined(side, own, other):
        return jnp.where(side == 0, jnp.concatenate([own, other]), jnp.concatenate([other, own]))

    def shift(array):
        return lax.ppermute(array, "subset", [(i, (i + 1) % subset_count) for i in range(subset_count)])

    def after(array, value):
        return lax.optimization_barrier((array, value))[0]

    rows = jnp.concatenate([tile_vox, tile_ray, jnp.broadcast_to(live_blocks, tile_vox.shape)], axis=0)
    own_index = jnp.pad(rows, ((0, 5), (0, -slots % LANES)))
    tiles = ((own_tiles,), (swap_cores(own_tiles),))
    held = (images, swap_cores(images))
    first_index = (own_index, swap_cores(own_index))

    def merged(own, other):
        return jnp.concatenate([own[:3], other[:3], jnp.zeros_like(own[:2])])

    index = merged(*first_index)
    dealt = (counts[0], swap_cores(counts[0]))

    def sensitivity(index, tiles):
        return call(sensitivity_kernel, {"index": index, "tiles": tiles},
                    {"inverse": shaped((both, 8, size), f32)},
                    [pltpu.VMEM((both, 8, size), f32)])["inverse"]

    sets = [(index, tiles, sensitivity(index, tiles))] * ROUNDS
    moves = [True] * (ROUNDS - 1)
    known = [None] * ROUNDS
    two = subset_count == 2 and ray_blocks <= 256 and slots <= size and size == LANES
    late = slots * 19 // 32
    if two:
        moves = [r == 0 for r in range(ROUNDS - 1)]

    low_scratch, back_scratch = pltpu.VMEM((both, half, size), bf16), pltpu.VMEM((both, half, size), f32)
    ray_scratch, sum_scratch = (pltpu.VMEM((ray_blocks, half, size), kind) for kind in (bf16, f32))
    piece = shaped((half, voxels), f32)
    summed = shaped((ray_blocks, half, size), f32)

    def only(k, pair):
        return tuple(value if i == k else None for i, value in enumerate(pair))

    def sums(r):
        fresh = known[r] is None
        sent = ray_blocks + fresh * rb_dev * CORES
        return ({"dealt": dealt} if fresh else {},
                {"wide": summed, "sent": shaped((sent, half, size), bf16)})

    extra, outs = sums(0)
    out = call(first_kernel, {"held": held, "index": first_index, "own_hbm": own_tiles, "tiles": tiles[1], **extra},
               outs, [low_scratch, sum_scratch, pltpu.VMEM(own_tiles.shape, bf16), pltpu.SemaphoreType.DMA])
    for r in range(ROUNDS):
        wide, sent = out["wide"], out["sent"]
        if two and r == 0:
            tiles_then, rows_then = after((own_tiles[late:], own_index), sent)
            slot = jnp.pad(rows_then.astype(bf16), ((0, size - 8), (0, 0)))[None]
            far_second = shift(jnp.concatenate([tiles_then, slot]))
        if two and r == 1:
            other_second = swap_cores(after(far_second, sent))
        for masks in steps:
            got = [swap_chips(sent, mask) for mask in masks]
            if masks is not steps[-1]:
                wide = wide + sum(part[:ray_blocks].astype(f32) for part in got)
                own, counted = place(masks), wide.astype(bf16)
                if sent.shape[0] > ray_blocks:
                    parts = dict(zip((0,) + masks, [sent] + got))
                    ordered = [parts[m * min(masks)][ray_blocks:] for m in range(len(parts))]
                    if len(ordered) == 2:
                        passed = joined(own, *ordered)
                    else:
                        passed = jnp.concatenate([lax.dynamic_index_in_dim(
                            jnp.stack(ordered), own ^ v, 0, keepdims=False) for v in range(len(ordered))])
                    counted = jnp.concatenate([counted, passed])
                sent = counted
        if two and r == 1:
            other_first = swap_cores(after(far_first, tuple(got)))
            far_tiles = ((far_first, far_second), (other_first, other_second))
            far_index = merged(*(piece[-1, :8].astype(jnp.int32) for piece in (far_second, other_second)))
            far = (far_index, far_tiles, sensitivity(far_index, far_tiles))
            sets = [far if later >= 2 and later % 2 == 0 else sets[later] for later in range(ROUNDS)]
        now_index, now_tiles, now_inverse = sets[r]
        base = {"index": now_index, "inverse": now_inverse}
        ins = {"wide": wide, "got": got, **base}
        outs = {}
        if known[r] is None:
            ins["sent"] = sent
            if two:
                outs["counts"] = summed.update(dtype=bf16)
        else:
            ins["counts"] = known[r]
        kernel = functools.partial(update_kernel, masks, r)
        last = r + 1 == ROUNDS
        if last or moves[r]:
            order = (1, 0) if last else (0, 1)
            moved, ratios = {}, None
            for k in order:
                if ratios is None:
                    out = call(kernel, {**ins, "held": only(k, held), "tiles": only(k, now_tiles)},
                               {"held": only(k, (piece,) * CORES), "ratios": summed.update(dtype=bf16), **outs},
                               [back_scratch, ray_scratch, ray_scratch])
                    ratios = out["ratios"]
                    if two and r == 0:
                        far_counts = shift(out["counts"])
                else:
                    out = {**out, **call(kernel, {**base, "ratios": ratios, "held": only(k, held),
                                                  "tiles": only(k, now_tiles)},
                                         {"held": only(k, (piece,) * CORES)}, [back_scratch])}
                moved[k] = out["held"][k]
                if two and r == 0 and k == 1:
                    far_first = shift(after(own_tiles[:late], moved[k]))
                if not last:
                    moved[k] = shift(moved[k])
                elif k == 1:
                    moved[k] = swap_cores(moved[k])
            if two and r == 0:
                moved[1], far_second = lax.optimization_barrier((moved[1], far_second))
            held = (moved[0], moved[1])
            if not last:
                extra, more = sums(r + 1)
                begun = call(functools.partial(project_kernel, r + 1), {"held": only(0, held), "index": sets[r + 1][0],
                                              "tiles": only(0, sets[r + 1][1])},
                             {"wide": summed}, [low_scratch, sum_scratch])["wide"]
                out = call(functools.partial(project_kernel, r + 1), {"held": only(1, held), "index": sets[r + 1][0], "begun": begun,
                                            "tiles": only(1, sets[r + 1][1]), **extra},
                           more, [low_scratch, sum_scratch])
        else:
            if two and r == 1:
                known[r + 1] = far_counts
            extra, more = sums(r + 1)
            ins.update(held=held, tiles=now_tiles)
            outs.update(held=(piece,) * CORES)
            if two and r == 1:
                out = call(kernel, ins, outs, [back_scratch, ray_scratch, ray_scratch])
                then = call(functools.partial(project_kernel, r + 1),
                            {"held": out["held"], "index": sets[r + 1][0], "tiles": sets[r + 1][1], **extra},
                            more, [low_scratch, sum_scratch])
                out = {**out, **then}
            else:
                ins.update(next_index=sets[r + 1][0], next_tiles=sets[r + 1][1], **extra)
                outs.update(more)
                out = call(kernel, ins, outs, [back_scratch, ray_scratch, ray_scratch, low_scratch, sum_scratch])
            held = out["held"]
            if two and r == 1:
                known = [known[later] if later < 2 else far_counts if later % 2 == 0 else out["counts"]
                         for later in range(ROUNDS)]
    return joined(core, held[0], held[1])


def solution(mesh):
    in_specs = (
        P("subset", "tile"),
        P("subset", "tile", None, None),
        P("subset", "tile"),
        P("subset", "tile"),
        P("subset", "tile"),
        P("subset", None, "tile"),
    )
    return jax.shard_map(shards, mesh=mesh, in_specs=in_specs, out_specs=P("subset", "tile"),
                         check_vma=False)
```
